256 devices in a mesh: sub: 32 (over y, x, core), row: 8 (over z).
Axes of the slice: x: 4, y: 4, z: 8, core: 2. Of those that a mesh axis runs over, the one named last changes fastest.
Arguments:
- source: bfloat16 [4, 32, 4096, 256], P(None, 'sub', 'row'), may hold values from -6 to 6
- inverse_z: bfloat16 [32, 4096, 4096], P('sub', 'row'), may hold values from -1 to 2
- pattern: int32 [32, 16, 16], P('sub', 'row'), may hold values from 0 to 1, as said below
- line_far: int32 [32, 1024, 2], P('sub', 'row'), may hold values from 0 to 1023, as said below
- delay: int32 [32, 1024], P('sub', 'row'), may hold values from 1 to 2, as said below
- xf_node: int32 [32, 64], P('sub', 'row'), may hold values from 0 to 4095, as said below
- wave0: bfloat16 [2, 32, 1024, 256], P(None, 'sub', 'row'), may hold values from -6 to 6
- flux0: float32 [32, 64, 256], P('sub', 'row'), may hold values from -6 to 6
- volt0: float32 [32, 64, 256], P('sub', 'row'), may hold values from -6 to 6
- slope: float32 [4], replicated, may hold values from 0.1 to 1.5
- knee: float32 [3], replicated, may hold values from 0.4 to 2.5
Outputs:
- voltage: float32 [32, 4096, 256], P('sub', 'row')
- flux_state: float32 [32, 64, 256], P('sub', 'row')
The draws below stay inside these ranges and needn't reach their ends.
Inputs may be any that keep to these rules, and one draw needn't show every extreme that they name: Each pattern has all diagonal blocks present. `line_far`: pairs line ends: the far end of the far end is the line end itself, in another subnetwork, in the same block of 128 line ends; at most 6 line ends of one block lead to one far subnetwork, and that many do in every draw. Both ends of a line have the same delay. `xf_node`: transformer j sits at a node of the same block of 512 nodes as j // 8, never at a line end's node.
All inputs are finite; a program needn't handle non-finite values.
Results may differ from the reference program's by a relative error of at most 0.0055.
Values may be sent and summed in bfloat16 or wider, within the bound.
A program may use at most 64 MiB of HBM per device.

```python
import math
import jax
import jax.numpy as jnp
from jax import lax

NODES = 4096
BLOCK = 256
PORT_DEV = 128
XF_DEV = 8
SEGS = 4
STEPS = 4
SCEN = 256
NSUB = 32
BLOCKS = 16
ROWS_DEV = 512
PORTS = 1024
XF = 64


def permute_one(subkey):
    return jax.random.permutation(subkey, NSUB - 1)


def shared_lines(key):
    slots = PORTS // PORT_DEV
    groups = PORT_DEV // 2
    key_perm, key_swap, key_delay = jax.random.split(key, 3)
    orders = jax.vmap(permute_one)(jax.random.split(key_perm, slots))
    masks = 1 + orders[:, jnp.arange(groups) % (NSUB - 1)]
    swapped = jax.random.randint(key_swap, (slots, groups), 0, 2)
    delays = jax.random.randint(key_delay, (slots, groups), 1, 3)
    shape = (NSUB, slots, groups, 2)
    subnet_ids = jnp.arange(NSUB, dtype=jnp.int32).reshape(NSUB, 1, 1, 1)
    member = jnp.arange(2, dtype=jnp.int32).reshape(1, 1, 1, 2)
    far_subnet = jnp.broadcast_to(jnp.bitwise_xor(subnet_ids, masks[None, :, :, None]), shape)
    far_member = jnp.bitwise_xor(member, swapped[None, :, :, None])
    slot_base = jnp.arange(slots, dtype=jnp.int32).reshape(1, slots, 1, 1) * PORT_DEV
    group_base = 2 * jnp.arange(groups, dtype=jnp.int32).reshape(1, 1, groups, 1)
    far_port = jnp.broadcast_to(slot_base + group_base + far_member, shape)
    far_all = jnp.stack([far_subnet, far_port], -1).reshape(NSUB, PORTS, 2)
    delay_all = jnp.broadcast_to(delays[None, :, :, None], shape).reshape(NSUB, PORTS)
    return (far_all, delay_all)


def draw_line_far(key, part):
    far_all, delay_all = shared_lines(key)
    return far_all.astype(jnp.int32)


def draw_delay(key, part):
    far_all, delay_all = shared_lines(key)
    return delay_all.astype(jnp.int32)


def draw_pattern(key, part):
    key = jax.random.fold_in(key, 7)
    present = jax.random.randint(key, (NSUB, BLOCKS, BLOCKS), 0, 2)
    diagonal = jnp.eye(BLOCKS, dtype=jnp.int32)[None]
    return jnp.maximum(present, diagonal).astype(jnp.int32)


def draw_xf_node(key, part):
    key = jax.random.fold_in(key, 11)
    local = jax.random.randint(key, (NSUB, XF), PORT_DEV, ROWS_DEV)
    base = jnp.arange(XF, dtype=jnp.int32) // XF_DEV * ROWS_DEV
    return (base[None, :] + local).astype(jnp.int32)


def draw_inverse_z(key, part):
    key = jax.random.fold_in(key, 5)
    key_off, key_diag = jax.random.split(key)
    spread = jnp.clip(jax.random.normal(key_off, (NSUB, NODES, NODES), jnp.float32), -4.0, 4.0)
    spread = spread / math.sqrt(NODES)
    diagonal = jax.random.uniform(key_diag, (NSUB, NODES), jnp.float32, 0.8, 1.6)
    identity = jnp.eye(NODES, dtype=jnp.float32)[None]
    return (spread * (1.0 - identity) + identity * diagonal[:, :, None]).astype(jnp.bfloat16)


def shard_levels(stream_key, shape, cuts, least, high):
    def one(position, parts):
        draws = jax.random.uniform(jax.random.fold_in(jax.random.fold_in(stream_key, 6), position), (parts,), jnp.float32, least / len(cuts), high / len(cuts))
        return jnp.repeat(jnp.exp(draws), shape[position] // parts).reshape((-1,) + (1,) * (len(shape) - position - 1))

    factor_of = one(*cuts[0])
    for cut in cuts[1:]:
        factor_of = factor_of * one(*cut)
    return factor_of


def scatter_about(key, extent, deviation, bound, cuts=(), held_as=jnp.bfloat16):
    entries = jax.random.normal(key, extent, jnp.float32) * deviation
    if len(cuts) > 0:
        entries = shard_levels(key, extent, cuts, -0.22, 0.18) * entries
    return jnp.clip(entries, min=-bound, max=bound).astype(held_as)


def setup_inputs(seed: int = 0) -> dict:
    arg_keys = jax.random.split(jax.random.key(seed), 12)
    return {
        "source": scatter_about(arg_keys[0], (STEPS, NSUB, NODES, SCEN), 1.0, 6.0, ((1, 32), (2, 8))),
        "inverse_z": draw_inverse_z(jax.random.fold_in(arg_keys[11], 71), 0),
        "pattern": draw_pattern(jax.random.fold_in(arg_keys[11], 71), 0),
        "line_far": draw_line_far(jax.random.fold_in(arg_keys[11], 71), 0),
        "delay": draw_delay(jax.random.fold_in(arg_keys[11], 71), 0),
        "xf_node": draw_xf_node(jax.random.fold_in(arg_keys[11], 71), 0),
        "wave0": scatter_about(arg_keys[6], (2, NSUB, PORTS, SCEN), 1.0, 6.0, ((1, 32), (2, 8))),
        "flux0": scatter_about(arg_keys[7], (NSUB, XF, SCEN), 1.0, 6.0, ((0, 32), (1, 8)), jnp.float32),
        "volt0": scatter_about(arg_keys[8], (NSUB, XF, SCEN), 1.0, 6.0, ((0, 32), (1, 8)), jnp.float32),
        "slope": jnp.clip(jnp.exp(jax.random.uniform(arg_keys[9], (SEGS,), jnp.float32, math.log(0.1), math.log(1.5))), 0.1, 1.5),
        "knee": jnp.clip(jnp.exp(jax.random.uniform(arg_keys[10], (SEGS - 1,), jnp.float32, math.log(0.4), math.log(2.5))), 0.4, 2.5),
    }


def expand_mask(block_mask, block_size):
    return jnp.repeat(jnp.repeat(block_mask, block_size, 0), block_size, 1)


def solve_one(operands):
    impedance, block_mask, injection_total = operands
    keep = expand_mask(block_mask, BLOCK) > 0
    masked = jnp.where(keep, impedance.astype(jnp.float32), jnp.float32(0.0))
    return jnp.dot(masked, injection_total, precision=lax.Precision.HIGHEST)


def saturation(flux_now, slope, knee):
    magnitude = jnp.abs(flux_now)
    direction = jnp.sign(flux_now)
    current = slope[0] * flux_now
    for level in range(SEGS - 1):
        current = current + slope[level + 1] * direction * jnp.maximum(magnitude - knee[level], 0.0)
    return current


def reference(source, inverse_z, pattern, line_far, delay, xf_node, wave0, flux0, volt0, slope, knee):
    port_ids = jnp.arange(PORTS, dtype=jnp.int32)
    port_nodes = (port_ids // PORT_DEV) * ROWS_DEV + port_ids % PORT_DEV
    subnet_ids = jnp.arange(NSUB, dtype=jnp.int32)[:, None]
    far_subnet = line_far[:, :, 0]
    far_port = line_far[:, :, 1]
    delayed = (delay == 2)[:, :, None]
    recent = wave0[0]
    earlier = wave0[1]
    flux_state = flux0
    xf_previous = volt0
    voltage = jnp.zeros((NSUB, NODES, SCEN), jnp.float32)
    for instant in range(STEPS):
        arriving = jnp.where(delayed, earlier, recent)
        current = saturation(flux_state, slope, knee)
        absorbed = jnp.zeros((NSUB, NODES, SCEN), jnp.float32).at[subnet_ids, xf_node].add(current)
        inject = (source[instant].astype(jnp.float32) - absorbed).astype(jnp.bfloat16)
        injection_total = inject.astype(jnp.float32).at[:, port_nodes].add(arriving.astype(jnp.float32))
        voltage = lax.map(solve_one, (inverse_z, pattern, injection_total))
        xf_voltage = voltage[subnet_ids, xf_node]
        flux_state = flux_state + 0.5 * (xf_voltage + xf_previous)
        xf_previous = xf_voltage
        if instant + 1 < STEPS:
            outgoing = (0.5 * voltage[:, port_nodes] - arriving.astype(jnp.float32)).astype(jnp.bfloat16)
            incoming = outgoing[far_subnet, far_port]
            earlier = recent
            recent = incoming
    return voltage, flux_state
```

```python
import functools

import jax
import jax.numpy as jnp
from jax import lax
from jax.experimental import pallas as pl
from jax.experimental.pallas import tpu as pltpu
from jax.sharding import PartitionSpec as P

MESH = pl.DeviceIdType.MESH
BF = jnp.bfloat16
F32 = jnp.float32
HALF = 128
SLOTS = 8


def dot(a, b):
    return jnp.dot(a, b, preferred_element_type=F32)


def dot_t(a, b):
    return lax.dot_general(a, b, (((1,), (1,)), ((), ())), preferred_element_type=F32)


def kernel(
    n_sub, n_row, rows, ports, xfs, steps, block,
    source, z, pattern, far, delay, xf, wave0, flux0, volt0, slope, knee,
    vout, fout,
    zm, src, zc, zx, stat, y, rs_send, rs_recv, xs, xr, pk, un, s3, d3, zx3, xfi, xfr, vacc, wrec, wear, warr, cur,
    load_sem, z_send, z_recv, rs_ssem, rs_rsem, x_ssem, x_rsem, s3_ssem, s3_rsem, d3_ssem, d3_rsem, i_ssem, i_rsem,
):
    me = lax.axis_index("row")
    sub = lax.axis_index("sub")
    last = steps - 1
    other = rows - ports
    xr2 = 2 * xfs
    prow = ports + xr2
    scen = 2 * HALF
    n_hop = n_row // 2

    def at_row(d):
        return (sub, lax.rem(me + d + 2 * n_row, n_row))

    def row_of(d):
        return lax.rem(me + d + 2 * n_row, n_row)

    def remote(a, b, ss, rs, dev):
        return pltpu.make_async_remote_copy(
            src_ref=a, dst_ref=b, send_sem=ss, recv_sem=rs, device_id=dev, device_id_type=MESH
        )

    ld_ports = pltpu.make_async_copy(z.at[pl.ds(0, ports)], zm.at[pl.ds(0, ports)], load_sem.at[0])
    ld_rest = pltpu.make_async_copy(z.at[pl.ds(ports, other)], zm.at[pl.ds(ports, other)], load_sem.at[1])
    ld_src = pltpu.make_async_copy(source, src, load_sem.at[2])
    ld_ports.start()
    ld_rest.start()
    ld_src.start()
    barrier = pltpu.get_barrier_semaphore()
    for d in range(1, n_row):
        pl.semaphore_signal(barrier, inc=1, device_id=at_row(d), device_id_type=MESH)

    def greet(i, c):
        pl.semaphore_signal(
            barrier, inc=1, device_id=(lax.rem(sub + i, n_sub), me), device_id_type=MESH
        )
        return c

    lax.fori_loop(1, n_sub, greet, 0)

    ri = lax.broadcasted_iota(jnp.int32, (xr2, rows), 0)
    li = lax.broadcasted_iota(jnp.int32, (xr2, rows), 1)
    oh = jnp.zeros((xr2, rows), F32)
    bi = lax.broadcasted_iota(jnp.int32, (xfs, 128), 0)
    idx = jnp.zeros((xfs, 128), jnp.int32)
    for j in range(xfs):
        node = xf[0, j] & (rows - 1)
        oh = jnp.where((lax.rem(ri, xfs) == j) & (li == node), 1.0, oh)
        idx = jnp.where(bi == j, node, idx)
    oh = oh.astype(BF)
    node_col = idx[:, 0:1]
    node_row = jnp.zeros((1, xfs), jnp.int32)
    lane = lax.broadcasted_iota(jnp.int32, (1, xfs), 1)
    for j in range(xfs):
        node_row = jnp.where(lane == j, xf[0, j] & (rows - 1), node_row)
    shared = node_col == node_row
    ahead = lax.broadcasted_iota(jnp.int32, (xfs, xfs), 1) < lax.broadcasted_iota(jnp.int32, (xfs, xfs), 0)
    first = jnp.sum(jnp.where(shared & ahead, 1, 0), axis=1, keepdims=True) == 0
    xfi[...] = idx
    xfr[me] = idx

    def mask_rows(lo, count, brow):
        def one(b, c):
            m = jnp.where(pattern[brow, b] > 0, 1.0, 0.0).astype(F32)
            mv = jnp.full((1, block), m, F32).astype(BF)
            cols = pl.ds(pl.multiple_of(b * block, block), block)
            zm[lo : lo + count, cols] = zm[lo : lo + count, cols] * mv
            return c

        lax.fori_loop(0, n_row * rows // block, one, 0)

    ld_ports.wait()
    mask_rows(0, ports, 0)
    ld_rest.wait()
    mask_rows(ports, block - ports, 0)
    for b in range(1, rows // block):
        mask_rows(b * block, block, b)

    def pick(c, carry):
        cols = pl.ds(pl.multiple_of(c * rows, rows), rows)
        zm[rows : rows + xr2, cols] = dot(oh, zm[0:rows, cols]).astype(BF)
        return carry

    lax.fori_loop(0, n_row, pick, 0)

    pl.semaphore_wait(barrier, n_row - 1 + n_sub - 1)

    order = [n_hop]
    for d in range(n_hop - 1, 0, -1):
        order += [d, n_row - d]
    z_copies = {}
    for d in order:
        cols = pl.ds(pl.multiple_of(row_of(d) * rows, rows), rows)
        a = remote(zm.at[pl.ds(0, ports), cols], zc.at[me, pl.ds(0, ports)], z_send.at[0, d], z_recv.at[0, d], at_row(d))
        b = remote(zm.at[pl.ds(rows, xr2), cols], zc.at[me, pl.ds(ports, xr2)], z_send.at[1, d], z_recv.at[1, d], at_row(d))
        a.start()
        b.start()
        z_copies[d] = (a, b)
    i_copies = []
    for d in range(1, n_row):
        c = remote(xfi, xfr.at[me], i_ssem.at[d], i_rsem.at[d], at_row(d))
        c.start()
        i_copies.append(c)

    eye = lax.broadcasted_iota(jnp.int32, (ports, ports), 0) == lax.broadcasted_iota(jnp.int32, (ports, ports), 1)
    before = lax.broadcasted_iota(jnp.int32, (ports, ports), 0) < lax.broadcasted_iota(jnp.int32, (ports, ports), 1)
    fs_col = far[:, 0:1]
    fp_col = far[:, 1:2]
    fs_row = jnp.sum(jnp.where(eye, fs_col, 0), axis=0, keepdims=True)
    fp_row = jnp.sum(jnp.where(eye, fp_col, 0), axis=0, keepdims=True)
    same = fs_col == fs_row
    rank_row = jnp.sum(jnp.where(same & before, 1, 0), axis=0, keepdims=True)
    rank_col = jnp.sum(jnp.where(same & (fp_row < fp_col), 1, 0), axis=1, keepdims=True)
    dl_col = jnp.sum(jnp.where(eye, delay[...], 0), axis=1, keepdims=True)
    late = dl_col == 2
    n_slot = 2 * SLOTS * n_sub
    place_row = fs_row * (2 * SLOTS) + rank_row
    place_col = fs_col * (2 * SLOTS) + rank_col
    for h in range(2):
        pi = lax.broadcasted_iota(jnp.int32, (n_slot, ports), 0)
        pk[:, h * ports : (h + 1) * ports] = jnp.where(pi == place_row + h * SLOTS, 1.0, 0.0).astype(BF)
        ui = lax.broadcasted_iota(jnp.int32, (ports, n_slot), 1)
        un[h * ports : (h + 1) * ports, :] = jnp.where(ui == place_col + h * SLOTS, 1.0, 0.0).astype(BF)
    own_slots = pl.ds(pl.multiple_of(sub * 2 * SLOTS, 2 * SLOTS), 2 * SLOTS)
    for t in range(last):
        xr[t, own_slots, :] = jnp.zeros((2 * SLOTS, HALF), BF)

    wrec[...] = wave0[0].astype(F32)
    wear[...] = wave0[1].astype(F32)

    def currents(flux, at_xf):
        total = slope[0] * flux
        for level in range(3):
            total = total + slope[level + 1] * (
                jnp.maximum(flux - knee[level], 0.0) + jnp.minimum(flux + knee[level], 0.0)
            )
        absorbed = jnp.zeros_like(total)
        for j in range(xfs):
            absorbed = absorbed + jnp.where(shared[:, j : j + 1], total[j : j + 1], 0.0)
        inject = (at_xf - absorbed).astype(BF).astype(F32)
        delta = jnp.where(first, inject - at_xf, 0.0)
        high = delta.astype(BF).astype(F32)
        return jnp.concatenate([high, delta - high], axis=0)

    def begin(t, flux):
        warr[...] = jnp.where(late, wear[...], wrec[...])
        cur[...] = currents(flux, dot(oh, src[t])[0:xfs]).astype(BF)

    flux = flux0[...]
    xprev = volt0[...]
    ld_src.wait()
    begin(0, flux)

    own_cols = pl.ds(pl.multiple_of(me * rows, rows), rows)
    zc[me, 0:ports] = zm[0:ports, own_cols]
    zc[me, ports:prow] = zm[rows : rows + xr2, own_cols]
    s3[me] = src[last, ports:rows, :]

    def products(r):
        zr = zc[r]
        zx[r] = dot_t(zr, oh).astype(BF)
        for t in range(last):
            stat[t, r] = dot(zr, src[t])

    def add_dynamic(t, r):
        y[r] = stat[t, r] + dot(zc[r, :, 0:ports], warr[...].astype(BF)) + dot(zx[r], cur[...])

    first_dir = jnp.where(lax.rem(me, n_hop) < n_hop // 2, 1, 0)

    def both(v):
        v = v.astype(F32)
        return v[0:xfs] + v[xfs:]

    def reduce_scatter(t, ready):
        copies = []

        def push(dirn, sign, dest, k, h, wait):
            lanes = pl.ds(pl.multiple_of(h * HALF, HALF), HALF)
            acc_p = y[dest, 0:ports, lanes]
            acc_x = y[dest, ports : ports + xfs, lanes]
            if wait:
                got = rs_recv.at[t, dirn, k - 1, h]
                remote(got, got, rs_ssem.at[t, dirn, k - 1, h], rs_rsem.at[t, dirn, k - 1, h], at_row(sign)).wait_recv()
                acc_p = acc_p + got[0:ports].astype(F32)
                acc_x = acc_x + both(got[ports:prow])
            high = acc_x.astype(BF).astype(F32)
            rs_send[t, dirn, k, h, 0:ports] = acc_p.astype(BF)
            rs_send[t, dirn, k, h, ports:prow] = jnp.concatenate([high, acc_x - high], axis=0).astype(BF)
            c = remote(
                rs_send.at[t, dirn, k, h], rs_recv.at[t, dirn, k, h], rs_ssem.at[t, dirn, k, h], rs_rsem.at[t, dirn, k, h], at_row(sign)
            )
            c.start()
            copies.append(c)

        for k in range(n_hop):
            ready(n_hop - k)
            for j in range(2):
                dirn = jnp.bitwise_xor(first_dir, j)
                sign = 1 - 2 * dirn
                dest = row_of(sign * (n_hop - k))
                if k == 0:
                    push(dirn, sign, dest, k, dirn, False)
                elif k == 1:
                    push(dirn, sign, dest, k, 1 - dirn, False)
            for j in range(2):
                dirn = jnp.bitwise_xor(first_dir, j)
                sign = 1 - 2 * dirn
                dest = row_of(sign * (n_hop - k))
                if k == 1:
                    push(dirn, sign, dest, k, dirn, True)
                elif k > 1:
                    for h in range(2):
                        push(dirn, sign, dest, k, h, True)
        ready(0)
        for dirn in range(2):
            for h in range(2):
                got = rs_recv.at[t, dirn, n_hop - 1, h]
                remote(
                    got, got, rs_ssem.at[t, dirn, n_hop - 1, h], rs_rsem.at[t, dirn, n_hop - 1, h], at_row(1)
                ).wait_recv()
        at_ports, at_xfs = [], []
        for h in range(2):
            lanes = slice(h * HALF, (h + 1) * HALF)
            left, right = rs_recv.at[t, 0, n_hop - 1, h], rs_recv.at[t, 1, n_hop - 1, h]
            at_ports.append(y[me, 0:ports, lanes] + left[0:ports].astype(F32) + right[0:ports].astype(F32))
            at_xfs.append(y[me, ports : ports + xfs, lanes] + both(left[ports:prow]) + both(right[ports:prow]))
        return at_ports, at_xfs, copies

    def gather_hop(buf, own, k, ssem, rsem, cut):
        made = []
        n = buf.shape[1]
        for dirn in range(2):
            sign = 1 - 2 * dirn
            c = row_of(-sign * k)
            if k < n_hop - 1:
                part = pl.ds(0, n)
            else:
                part = pl.ds(0, cut) if dirn == 0 else pl.ds(cut, n - cut)
            cp = remote(buf.at[c, part], buf.at[c, part], ssem.at[dirn, k], rsem.at[dirn, k], at_row(sign))
            cp.start()
            made.append(cp)
        return made

    def gather_wait(made):
        for cp in made:
            cp.wait_recv()

    def add_static(c):
        lo = pl.multiple_of(c * rows + ports, ports)
        vacc[...] += dot(zm[:, pl.ds(lo, other)], s3[c])

    def add_last(c):
        lo = pl.multiple_of(c * rows, rows)
        vacc[...] += dot(zm[:, pl.ds(lo, ports)], d3[c, 0:ports]) + dot(zx3[c], d3[c, ports:prow])

    sends = []
    s3_hops = []
    for t in range(last):
        if t == 0:

            def ready(d):
                for e in (d, n_row - d) if 0 < d < n_hop else (d,):
                    if e:
                        f = n_row - e
                        r = row_of(e)
                        remote(zc.at[r, pl.ds(0, ports)], zc.at[r, pl.ds(0, ports)], z_send.at[0, f], z_recv.at[0, f], at_row(1)).wait_recv()
                        remote(zc.at[r, pl.ds(ports, xr2)], zc.at[r, pl.ds(ports, xr2)], z_send.at[1, f], z_recv.at[1, f], at_row(1)).wait_recv()
                        products(r)
                        add_dynamic(0, r)

            products(me)
            add_dynamic(0, me)
        else:

            def ready(d, t=t):
                for e in (d, n_row - d) if 0 < d < n_hop else (d,):
                    add_dynamic(t, row_of(e))

        at_ports, at_xfs, copies = reduce_scatter(t, ready)
        sends += copies
        xv = jnp.concatenate(at_xfs, axis=1)
        flux = flux + 0.5 * (xv + xprev)
        xprev = xv
        out = jnp.concatenate(
            [(0.5 * at_ports[h] - warr[:, h * HALF : (h + 1) * HALF]) for h in range(2)], axis=0
        ).astype(BF)
        xs[t] = dot(pk[...], out).astype(BF)

        def put(i, c, t=t):
            p = lax.rem(sub + i, n_sub)
            remote(
                xs.at[t, pl.ds(pl.multiple_of(p * 2 * SLOTS, 2 * SLOTS), 2 * SLOTS)],
                xr.at[t, own_slots],
                x_ssem.at[t],
                x_rsem.at[t],
                (p, me),
            ).start()
            return c

        lax.fori_loop(1, n_sub, put, 0)
        if s3_hops:
            gather_wait(s3_hops[-1])
        s3_hops.append(gather_hop(s3, None, t, s3_ssem, s3_rsem, other // 2))
        if t == 0:
            vacc[...] = jnp.zeros_like(vacc)
            add_static(me)
            for d in range(1, n_row):
                c = row_of(-d)
                remote(xfr.at[c], xfr.at[c], i_ssem.at[d], i_rsem.at[d], at_row(1)).wait_recv()

            def columns(c, carry):
                node = xfr[c][:, 0:1]
                hot = jnp.where(lax.broadcasted_iota(jnp.int32, (xfs, rows), 1) == node, 1.0, 0.0)
                hot = jnp.concatenate([hot, hot], axis=0).astype(BF)
                cols = pl.ds(pl.multiple_of(c * rows, rows), rows)
                zx3[c] = dot_t(zm[:, cols], hot).astype(BF)
                return carry

            lax.fori_loop(0, n_row, columns, 0)
        else:
            add_static(row_of(-t))
            add_static(row_of(t))
        total = pl.ds(0, (n_sub - 1) * 2 * SLOTS)
        pltpu.make_async_copy(xs.at[t, total], xr.at[t, total], x_rsem.at[t]).wait()
        inc = dot(un[...], xr[t])
        wear[...] = wrec[...]
        wrec[...] = jnp.concatenate([inc[0:ports], inc[ports : 2 * ports]], axis=1)
        begin(t + 1, flux)

    d3[me, 0:ports] = (src[last, 0:ports, :].astype(F32) + warr[...]).astype(BF)
    d3[me, ports:prow] = cur[...]
    d3_hops = [gather_hop(d3, None, 0, d3_ssem, d3_rsem, 64)]
    gather_wait(s3_hops[-1])
    s3_hops.append(gather_hop(s3, None, n_hop - 1, s3_ssem, s3_rsem, other // 2))
    add_last(me)
    add_static(row_of(-(n_hop - 1)))
    add_static(row_of(n_hop - 1))
    for k in range(1, n_hop):
        gather_wait(d3_hops[-1])
        d3_hops.append(gather_hop(d3, None, k, d3_ssem, d3_rsem, 64))
        add_last(row_of(-k))
        add_last(row_of(k))
    gather_wait(s3_hops[-1])
    add_static(row_of(n_hop))
    gather_wait(d3_hops[-1])
    add_last(row_of(n_hop))
    vout[...] = vacc[0:rows]
    fout[...] = flux + 0.5 * (vacc[rows : rows + xfs] + xprev)

    for d in order:
        for cp in z_copies[d]:
            cp.wait_send()
    for cp in i_copies + sends:
        cp.wait_send()
    for made in s3_hops + d3_hops:
        for cp in made:
            cp.wait_send()
    for t in range(last):
        total = pl.ds(0, (n_sub - 1) * 2 * SLOTS)
        pltpu.make_async_copy(xs.at[t, total], xr.at[t, total], x_ssem.at[t]).wait()


def body(source, inverse_z, pattern, line_far, delay, xf_node, wave0, flux0, volt0, slope, knee):
    steps, _, rows, scen = source.shape
    nodes = inverse_z.shape[2]
    ports = line_far.shape[1]
    xfs = xf_node.shape[1]
    n_sub, n_row = lax.axis_size("sub"), lax.axis_size("row")
    block = nodes // pattern.shape[2]
    last = steps - 1
    xr2 = 2 * xfs
    prow = ports + xr2
    n_hop = n_row // 2
    other = rows - ports
    n_slot = 2 * SLOTS * n_sub
    vmem = pl.BlockSpec(memory_space=pltpu.VMEM)
    smem = pl.BlockSpec(memory_space=pltpu.SMEM)
    hbm = pl.BlockSpec(memory_space=pl.ANY)
    dma = pltpu.SemaphoreType.DMA
    voltage, flux = pl.pallas_call(
        functools.partial(kernel, n_sub, n_row, rows, ports, xfs, steps, block),
        out_shape=(
            jax.ShapeDtypeStruct((rows, scen), F32),
            jax.ShapeDtypeStruct((xfs, scen), F32),
        ),
        in_specs=[hbm, hbm, smem, vmem, vmem, smem, vmem, vmem, vmem, smem, smem],
        out_specs=(vmem, vmem),
        scratch_shapes=[
            pltpu.VMEM((rows + xr2, nodes), BF),
            pltpu.VMEM((steps, rows, scen), BF),
            pltpu.VMEM((n_row, prow, rows), BF),
            pltpu.VMEM((n_row, prow, xr2), BF),
            pltpu.VMEM((last, n_row, prow, scen), F32),
            pltpu.VMEM((n_row, prow, scen), F32),
            pltpu.VMEM((last, 2, n_hop, 2, prow, HALF), BF),
            pltpu.VMEM((last, 2, n_hop, 2, prow, HALF), BF),
            pltpu.VMEM((last, n_slot, HALF), BF),
            pltpu.VMEM((last, n_slot, HALF), BF),
            pltpu.VMEM((n_slot, 2 * ports), BF),
            pltpu.VMEM((2 * ports, n_slot), BF),
            pltpu.VMEM((n_row, other, scen), BF),
            pltpu.VMEM((n_row, prow, scen), BF),
            pltpu.VMEM((n_row, rows + xr2, xr2), BF),
            pltpu.VMEM((xfs, 128), jnp.int32),
            pltpu.VMEM((n_row, xfs, 128), jnp.int32),
            pltpu.VMEM((rows + xr2, scen), F32),
            pltpu.VMEM((ports, scen), F32),
            pltpu.VMEM((ports, scen), F32),
            pltpu.VMEM((ports, scen), F32),
            pltpu.VMEM((xr2, scen), BF),
            dma((3,)),
            dma((2, n_row)),
            dma((2, n_row)),
            dma((last, 2, n_hop, 2)),
            dma((last, 2, n_hop, 2)),
            dma((last,)),
            dma((last,)),
            dma((2, n_hop)),
            dma((2, n_hop)),
            dma((2, n_hop)),
            dma((2, n_hop)),
            dma((n_row,)),
            dma((n_row,)),
        ],
        compiler_params=pltpu.CompilerParams(
            collective_id=0, has_side_effects=True, vmem_limit_bytes=48 * 2**20
        ),
        name="grid_steps",
    )(
        source.reshape(steps, rows, scen),
        inverse_z.reshape(rows, nodes),
        pattern.reshape(pattern.shape[1:]),
        line_far.reshape(ports, 2),
        delay,
        xf_node,
        wave0.reshape(2, ports, scen),
        flux0.reshape(xfs, scen),
        volt0.reshape(xfs, scen),
        slope,
        knee,
    )
    return (voltage[None], flux[None])


def solution(mesh):
    return jax.shard_map(
        body,
        mesh=mesh,
        in_specs=(
            P(None, "sub", "row", None),
            P("sub", "row", None),
            P("sub", "row", None),
            P("sub", "row", None),
            P("sub", "row"),
            P("sub", "row"),
            P(None, "sub", "row", None),
            P("sub", "row", None),
            P("sub", "row", None),
            P(),
            P(),
        ),
        out_specs=(P("sub", "row", None), P("sub", "row", None)),
        check_vma=False,
    )
```

```python
import functools

import jax
import jax.numpy as jnp
from jax import lax
from jax.experimental import pallas as pl
from jax.experimental.pallas import tpu as pltpu
from jax.sharding import PartitionSpec as P

MESH = pl.DeviceIdType.MESH
BF = jnp.bfloat16
F32 = jnp.float32
HALF = 128
SLOTS = 8


def dot(a, b):
    return jnp.dot(a, b, preferred_element_type=F32)


def dot_t(a, b):
    return lax.dot_general(a, b, (((1,), (1,)), ((), ())), preferred_element_type=F32)


def kernel(
    n_sub, n_row, rows, ports, xfs, steps, block,
    source, z, pattern_in, far_in, delay_in, xf_in, wave0_in, flux0_in, volt0_in, slope_in, knee_in,
    vout, fout,
    pattern, far, delay, xf, wave0, flux0, volt0, slope, knee,
    zm, src, zxs, zc, zcx, zd, stat, y, rs_send, rs_recv, xs, xr, pk, un, s3, dyn, d3, zl, xfi, xfr, vacc, wrec, wear, warr,
    load_sem, in_sem, z_send, z_recv, rs_ssem, rs_rsem, x_ssem, x_rsem, s3_ssem, s3_rsem, d3_ssem, d3_rsem, i_ssem, i_rsem,
):
    me = lax.axis_index("row")
    sub = lax.axis_index("sub")
    last = steps - 1
    other = rows - ports
    xr2 = 2 * xfs
    prow = ports + xr2
    n_hop = n_row // 2

    def row_of(d):
        return lax.rem(me + d + 2 * n_row, n_row)

    def at_row(d):
        return (sub, row_of(d))

    def remote(a, b, ss, rs, dev):
        return pltpu.make_async_remote_copy(
            src_ref=a, dst_ref=b, send_sem=ss, recv_sem=rs, device_id=dev, device_id_type=MESH
        )

    def arrived(buf, rs):
        remote(buf, buf, rs, rs, at_row(1)).wait_recv()

    ld_ports = pltpu.make_async_copy(z.at[pl.ds(0, ports)], zm.at[pl.ds(0, ports)], load_sem.at[0])
    ld_rest = pltpu.make_async_copy(z.at[pl.ds(ports, other)], zm.at[pl.ds(ports, other)], load_sem.at[1])
    ld_src = pltpu.make_async_copy(source, src, load_sem.at[2])
    small = [
        pltpu.make_async_copy(a, b, in_sem.at[i])
        for i, (a, b) in enumerate(
            [
                (pattern_in, pattern), (xf_in, xf), (far_in, far), (delay_in, delay), (wave0_in, wave0),
                (flux0_in, flux0), (volt0_in, volt0), (slope_in, slope), (knee_in, knee),
            ]
        )
    ]
    small[0].start()
    ld_ports.start()
    barrier = pltpu.get_barrier_semaphore()

    def greet(i, c):
        pl.semaphore_signal(
            barrier, inc=1, device_id=(lax.rem(sub + i, n_sub), me), device_id_type=MESH
        )
        return c

    for d in range(1, n_row):
        pl.semaphore_signal(barrier, inc=1, device_id=at_row(d), device_id_type=MESH)
    lax.fori_loop(1, n_sub, greet, 0)
    ld_rest.start()
    ld_src.start()
    for cp in small[1:]:
        cp.start()

    def mask_rows(lo, count, brow):
        def one(b, c):
            m = jnp.where(pattern[brow, b] > 0, 1.0, 0.0).astype(F32)
            mv = jnp.full((1, block), m, F32).astype(BF)
            cols = pl.ds(pl.multiple_of(b * block, block), block)
            zm[lo : lo + count, cols] = zm[lo : lo + count, cols] * mv
            return c

        lax.fori_loop(0, n_row * rows // block, one, 0)

    small[0].wait()
    ld_ports.wait()
    mask_rows(0, ports, 0)

    pl.semaphore_wait(barrier, n_row - 1 + n_sub - 1)

    z_copies = []

    def send_ports(d):
        cols = pl.ds(pl.multiple_of(row_of(d) * rows, rows), rows)
        cp = remote(zm.at[pl.ds(0, ports), cols], zc.at[me, pl.ds(0, ports)], z_send.at[0, d], z_recv.at[0, d], at_row(d))
        cp.start()
        z_copies.append(cp)

    order = [n_hop]
    for d in range(n_hop - 1, 0, -1):
        order += [d, n_row - d]
    for d in order[:3]:
        send_ports(d)

    for cp in small[1:]:
        cp.wait()
    ri = lax.broadcasted_iota(jnp.int32, (xr2, rows), 0)
    li = lax.broadcasted_iota(jnp.int32, (xr2, rows), 1)
    oh = jnp.zeros((xr2, rows), F32)
    bi = lax.broadcasted_iota(jnp.int32, (xfs, 128), 0)
    lane = lax.broadcasted_iota(jnp.int32, (1, xfs), 1)
    idx = jnp.zeros((xfs, 128), jnp.int32)
    node_row = jnp.zeros((1, xfs), jnp.int32)
    for j in range(xfs):
        node = xf[0, j] & (rows - 1)
        oh = jnp.where((lax.rem(ri, xfs) == j) & (li == node), 1.0, oh)
        idx = jnp.where(bi == j, node, idx)
        node_row = jnp.where(lane == j, node, node_row)
    oh_cols = jnp.concatenate([oh, jnp.zeros((128 - xr2, rows), F32)], axis=0).astype(BF)
    oh = oh.astype(BF)
    xfi[...] = idx
    xfr[me] = idx
    shared = idx[:, 0:1] == node_row
    ahead = lax.broadcasted_iota(jnp.int32, (xfs, xfs), 1) < lax.broadcasted_iota(jnp.int32, (xfs, xfs), 0)
    first = jnp.sum(jnp.where(shared & ahead, 1, 0), axis=1, keepdims=True) == 0

    ld_rest.wait()
    mask_rows(ports, block - ports, 0)
    for b in range(1, rows // block):
        mask_rows(b * block, block, b)

    def pick(c, carry):
        cols = pl.ds(pl.multiple_of(c * rows, rows), rows)
        v = dot(oh, zm[0:rows, cols])
        zm[rows : rows + xr2, cols] = v.astype(BF)
        zxs[c] = jnp.concatenate([v[0:xfs, 0 : rows // 2], v[0:xfs, rows // 2 :]], axis=0).astype(BF)
        return carry

    lax.fori_loop(0, n_row, pick, 0)
    for d in order:
        cp = remote(zxs.at[row_of(d)], zcx.at[me], z_send.at[1, d], z_recv.at[1, d], at_row(d))
        cp.start()
        z_copies.append(cp)
        cp = remote(xfi, xfr.at[me], i_ssem.at[d], i_rsem.at[d], at_row(d))
        cp.start()
        z_copies.append(cp)
    for d in order[3:]:
        send_ports(d)

    eye = lax.broadcasted_iota(jnp.int32, (ports, ports), 0) == lax.broadcasted_iota(jnp.int32, (ports, ports), 1)
    before = lax.broadcasted_iota(jnp.int32, (ports, ports), 0) < lax.broadcasted_iota(jnp.int32, (ports, ports), 1)
    fs_row = far[0:1, :]
    fp_row = far[1:2, :]
    fs_col = jnp.sum(jnp.where(eye, fs_row, 0), axis=1, keepdims=True)
    fp_col = jnp.sum(jnp.where(eye, fp_row, 0), axis=1, keepdims=True)
    same = fs_col == fs_row
    rank_row = jnp.sum(jnp.where(same & before, 1, 0), axis=0, keepdims=True)
    rank_col = jnp.sum(jnp.where(same & (fp_row < fp_col), 1, 0), axis=1, keepdims=True)
    dl_col = jnp.sum(jnp.where(eye, delay[...], 0), axis=1, keepdims=True)
    late = dl_col == 2
    n_slot = 2 * SLOTS * n_sub
    place_row = fs_row * (2 * SLOTS) + rank_row
    place_col = fs_col * (2 * SLOTS) + rank_col
    for h in range(2):
        pi = lax.broadcasted_iota(jnp.int32, (n_slot, ports), 0)
        pk[:, h * ports : (h + 1) * ports] = jnp.where(pi == place_row + h * SLOTS, 1.0, 0.0).astype(BF)
        ui = lax.broadcasted_iota(jnp.int32, (ports, n_slot), 1)
        un[h * ports : (h + 1) * ports, :] = jnp.where(ui == place_col + h * SLOTS, 1.0, 0.0).astype(BF)
    own_slots = pl.ds(pl.multiple_of(sub * 2 * SLOTS, 2 * SLOTS), 2 * SLOTS)
    for t in range(last):
        xr[t, own_slots, :] = jnp.zeros((2 * SLOTS, HALF), BF)

    wrec[...] = wave0[0].astype(F32)
    wear[...] = wave0[1].astype(F32)
    dyn[...] = jnp.zeros_like(dyn)
    for c in range(n_row):
        d3[c, prow:] = jnp.zeros((d3.shape[1] - prow, d3.shape[2]), BF)

    def currents(flux, at_xf):
        total = slope[0] * flux
        for level in range(3):
            total = total + slope[level + 1] * (
                jnp.maximum(flux - knee[level], 0.0) + jnp.minimum(flux + knee[level], 0.0)
            )
        absorbed = jnp.zeros_like(total)
        for j in range(xfs):
            absorbed = absorbed + jnp.where(shared[:, j : j + 1], total[j : j + 1], 0.0)
        inject = (at_xf - absorbed).astype(BF).astype(F32)
        delta = jnp.where(first, inject - at_xf, 0.0)
        high = delta.astype(BF).astype(F32)
        return jnp.concatenate([high, delta - high], axis=0).astype(BF)

    ld_src.wait()
    at_xf = [dot(oh, src[t])[0:xfs] for t in range(steps)]

    def begin(t, flux):
        warr[...] = jnp.where(late, wear[...], wrec[...])
        cur = currents(flux, at_xf[t])
        if t < last:
            dyn[0:ports] = warr[...].astype(BF)
            dyn[ports:prow] = cur
        else:
            d3[me, 0:ports] = (src[last, 0:ports, :].astype(F32) + warr[...]).astype(BF)
            d3[me, ports:prow] = cur

    flux = flux0[...]
    xprev = volt0[...]
    begin(0, flux)

    zc[me, 0:ports] = zm[0:ports, pl.ds(pl.multiple_of(me * rows, rows), rows)]
    zcx[me] = zxs[me]
    s3[me] = src[last, ports:rows, :]

    def products(r):
        v = zcx[r].astype(F32)
        v = jnp.concatenate([v[0:xfs], v[xfs:]], axis=1)
        zc[r, ports:prow] = jnp.concatenate([v, jnp.zeros_like(v)], axis=0).astype(BF)
        zr = zc[r]
        zd[r, :, 0:ports] = zc[r, :, 0:ports]
        zd[r, :, ports:] = dot_t(zr, oh_cols).astype(BF)
        y[r] = dot(zr, src[0]) + dot(zd[r], dyn[...])
        for t in range(1, last):
            stat[t - 1, r] = dot(zr, src[t])

    def add_dynamic(t, r):
        y[r] = stat[t - 1, r] + dot(zd[r], dyn[...])

    first_dir = jnp.where(lax.rem(me, n_hop) < n_hop // 2, 1, 0)

    def both_ways(f):
        for j in range(2):
            dirn = jnp.bitwise_xor(first_dir, j)
            f(dirn, 1 - 2 * dirn)

    def both(v):
        v = v.astype(F32)
        return v[0:xfs] + v[xfs:]

    sends = []

    def reduce_scatter(t, ready):
        def push(dirn, dest, slot, h, to, got):
            lanes = pl.ds(pl.multiple_of(h * HALF, HALF), HALF)
            acc_p = y[dest, 0:ports, lanes]
            acc_x = y[dest, ports : ports + xfs, lanes]
            for g in got:
                buf = rs_recv.at[t, dirn, g, h]
                arrived(buf, rs_rsem.at[t, dirn, g, h])
                acc_p = acc_p + buf[0:ports].astype(F32)
                acc_x = acc_x + both(buf[ports:prow])
            high = acc_x.astype(BF).astype(F32)
            rs_send[t, dirn, slot, h, 0:ports] = acc_p.astype(BF)
            rs_send[t, dirn, slot, h, ports:prow] = jnp.concatenate([high, acc_x - high], axis=0).astype(BF)
            cp = remote(
                rs_send.at[t, dirn, slot, h], rs_recv.at[t, dirn, slot, h],
                rs_ssem.at[t, dirn, slot, h], rs_rsem.at[t, dirn, slot, h], at_row(to),
            )
            cp.start()
            sends.append(cp)

        ready(4)
        both_ways(lambda dirn, sign: push(dirn, row_of(4 * sign), 0, dirn, 2 * sign, ()))
        ready(3)

        def second(dirn, sign):
            for h in range(2):
                push(dirn, row_of(3 * sign), 1, h, sign, ())

        both_ways(second)
        ready(2)

        def third(dirn, sign):
            push(dirn, row_of(2 * sign), 2, 1 - dirn, sign, (1,))
            push(dirn, row_of(2 * sign), 2, dirn, sign, (0, 1))

        both_ways(third)
        ready(1)

        def fourth(dirn, sign):
            for h in (1 - dirn, dirn):
                push(dirn, row_of(sign), 3, h, sign, (2,))

        both_ways(fourth)
        ready(0)
        at_ports, at_xfs = [], []
        for h in range(2):
            lanes = slice(h * HALF, (h + 1) * HALF)
            for dirn in range(2):
                arrived(rs_recv.at[t, dirn, 3, h], rs_rsem.at[t, dirn, 3, h])
            left, right = rs_recv.at[t, 0, 3, h], rs_recv.at[t, 1, 3, h]
            at_ports.append(y[me, 0:ports, lanes] + left[0:ports].astype(F32) + right[0:ports].astype(F32))
            at_xfs.append(y[me, ports : ports + xfs, lanes] + both(left[ports:prow]) + both(right[ports:prow]))
        return at_ports, at_xfs

    s3_cut = other // 2

    def s3_hop(k):
        for dirn in range(2):
            sign = 1 - 2 * dirn
            c = row_of(-sign * k)
            if k < n_hop - 1:
                part = pl.ds(0, other)
            else:
                part = pl.ds(dirn * s3_cut, s3_cut)
            cp = remote(s3.at[c, part], s3.at[c, part], s3_ssem.at[dirn, k], s3_rsem.at[dirn, k], at_row(sign))
            cp.start()
            sends.append(cp)

    def s3_wait(k):
        for dirn in range(2):
            part = pl.ds(0, other) if k < n_hop - 1 else pl.ds(0, s3_cut)
            arrived(s3.at[me, part], s3_rsem.at[dirn, k])

    def add_static(c):
        lo = pl.multiple_of(c * rows + ports, ports)
        vacc[...] += dot(zm[:, pl.ds(lo, other)], s3[c])

    def add_last(c):
        vacc[...] += dot(zl[c], d3[c])

    def columns(c, carry):
        node = xfr[c][:, 0:1]
        hot = jnp.where(lax.broadcasted_iota(jnp.int32, (xfs, rows), 1) == node, 1.0, 0.0)
        hot = jnp.concatenate([hot, hot, jnp.zeros((128 - xr2, rows), F32)], axis=0).astype(BF)
        zl[c, :, 0:ports] = zm[:, pl.ds(pl.multiple_of(c * rows, rows), ports)]
        zl[c, :, ports:] = dot_t(zm[:, pl.ds(pl.multiple_of(c * rows, rows), rows)], hot).astype(BF)
        return carry

    products(me)
    vacc[...] = jnp.zeros_like(vacc)
    add_static(me)
    for d in range(1, n_row):
        arrived(xfr.at[row_of(-d)], i_rsem.at[d])
    lax.fori_loop(0, n_row, columns, 0)

    for t in range(last):

        def ready(d, t=t):
            for e in (d, n_row - d) if 0 < d < n_hop else (d,):
                r = row_of(e)
                if t:
                    add_dynamic(t, r)
                elif e:
                    arrived(zc.at[r, pl.ds(0, ports)], z_recv.at[0, n_row - e])
                    arrived(zcx.at[r], z_recv.at[1, n_row - e])
                    products(r)

        at_ports, at_xfs = reduce_scatter(t, ready)
        xv = jnp.concatenate(at_xfs, axis=1)
        flux = flux + 0.5 * (xv + xprev)
        xprev = xv
        out = jnp.concatenate(
            [0.5 * at_ports[h] - warr[:, h * HALF : (h + 1) * HALF] for h in range(2)], axis=0
        ).astype(BF)
        xs[t] = dot(pk[...], out).astype(BF)

        def put(i, c, t=t):
            p = lax.rem(sub + i, n_sub)
            remote(
                xs.at[t, pl.ds(pl.multiple_of(p * 2 * SLOTS, 2 * SLOTS), 2 * SLOTS)],
                xr.at[t, own_slots],
                x_ssem.at[t],
                x_rsem.at[t],
                (p, me),
            ).start()
            return c

        lax.fori_loop(1, n_sub, put, 0)
        if t:
            s3_wait(t - 1)
        s3_hop(t)
        if t:
            add_static(row_of(-t))
            add_static(row_of(t))
        total = pl.ds(0, (n_sub - 1) * 2 * SLOTS)
        pltpu.make_async_copy(xs.at[t, total], xr.at[t, total], x_rsem.at[t]).wait()
        inc = dot(un[...], xr[t])
        wear[...] = wrec[...]
        wrec[...] = jnp.concatenate([inc[0:ports], inc[ports : 2 * ports]], axis=1)
        begin(t + 1, flux)

    parts = ((0, ports // 2), (ports // 2, prow - ports // 2))

    def d3_send(dirn, sign, slot, p, c, to):
        part = pl.ds(*parts[p])
        cp = remote(d3.at[c, part], d3.at[c, part], d3_ssem.at[dirn, slot, p], d3_rsem.at[dirn, slot, p], at_row(to))
        cp.start()
        sends.append(cp)

    def d3_wait(dirn, slot, p):
        arrived(d3.at[me, pl.ds(*parts[p])], d3_rsem.at[dirn, slot, p])

    for p in range(2):
        both_ways(lambda dirn, sign: d3_send(dirn, sign, 0, p, me, sign))
    add_last(me)
    s3_wait(n_hop - 2)
    s3_hop(n_hop - 1)
    for k in (1, 2):

        def forward(dirn, sign):
            for p in range(2):
                d3_wait(dirn, k - 1, p)
                d3_send(dirn, sign, k, p, row_of(-sign * k), sign)
                if k == 2:
                    @pl.when(dirn == p)
                    def _():
                        part = pl.ds(*parts[p])
                        c = row_of(-sign * k)
                        remote(
                            d3.at[c, part], d3.at[c, part], d3_ssem.at[dirn, 3, p], d3_rsem.at[dirn, 3, p], at_row(2 * sign)
                        ).start()

        both_ways(forward)
        add_last(row_of(-k))
        add_last(row_of(k))
        if k == 1:
            add_static(row_of(-(n_hop - 1)))
            add_static(row_of(n_hop - 1))
    s3_wait(n_hop - 1)
    add_static(row_of(n_hop))
    for p in range(2):
        both_ways(lambda dirn, sign: d3_wait(dirn, 2, p))
    add_last(row_of(-3))
    add_last(row_of(3))
    for p in range(2):
        d3_wait(p, 3, p)
    add_last(row_of(n_hop))
    out_copy = pltpu.make_async_copy(vacc.at[pl.ds(0, rows)], vout, load_sem.at[0])
    out_copy.start()
    flux0[...] = flux + 0.5 * (vacc[rows : rows + xfs] + xprev)
    flux_copy = pltpu.make_async_copy(flux0, fout, load_sem.at[1])
    flux_copy.start()

    for cp in z_copies + sends:
        cp.wait_send()
    for p in range(2):
        buf = d3.at[me, pl.ds(*parts[p])]
        remote(buf, buf, d3_ssem.at[p, 3, p], d3_rsem.at[p, 3, p], at_row(1)).wait_send()
    for t in range(last):
        total = pl.ds(0, (n_sub - 1) * 2 * SLOTS)
        pltpu.make_async_copy(xs.at[t, total], xr.at[t, total], x_ssem.at[t]).wait()
    out_copy.wait()
    flux_copy.wait()


def body(source, inverse_z, pattern, line_far, delay, xf_node, wave0, flux0, volt0, slope, knee):
    steps, _, rows, scen = source.shape
    nodes = inverse_z.shape[2]
    ports = line_far.shape[1]
    xfs = xf_node.shape[1]
    n_sub, n_row = lax.axis_size("sub"), lax.axis_size("row")
    block = nodes // pattern.shape[2]
    last = steps - 1
    xr2 = 2 * xfs
    prow = ports + xr2
    n_hop = n_row // 2
    other = rows - ports
    n_slot = 2 * SLOTS * n_sub
    hbm = pl.BlockSpec(memory_space=pltpu.HBM)
    dma = pltpu.SemaphoreType.DMA
    voltage, flux = pl.pallas_call(
        functools.partial(kernel, n_sub, n_row, rows, ports, xfs, steps, block),
        out_shape=(
            jax.ShapeDtypeStruct((rows, scen), F32),
            jax.ShapeDtypeStruct((xfs, scen), F32),
        ),
        in_specs=[hbm] * 11,
        out_specs=(hbm, hbm),
        scratch_shapes=[
            pltpu.SMEM(pattern.shape[1:], jnp.int32),
            pltpu.VMEM((2, ports), jnp.int32),
            pltpu.VMEM(delay.shape, jnp.int32),
            pltpu.SMEM(xf_node.shape, jnp.int32),
            pltpu.VMEM((2, ports, scen), BF),
            pltpu.VMEM((xfs, scen), F32),
            pltpu.VMEM((xfs, scen), F32),
            pltpu.SMEM(slope.shape, F32),
            pltpu.SMEM(knee.shape, F32),
            pltpu.VMEM((rows + xr2, nodes), BF),
            pltpu.VMEM((steps, rows, scen), BF),
            pltpu.VMEM((n_row, xr2, rows // 2), BF),
            pltpu.VMEM((n_row, prow, rows), BF),
            pltpu.VMEM((n_row, xr2, rows // 2), BF),
            pltpu.VMEM((n_row, prow, ports + 128), BF),
            pltpu.VMEM((last - 1, n_row, prow, scen), F32),
            pltpu.VMEM((n_row, prow, scen), F32),
            pltpu.VMEM((last, 2, 4, 2, prow, HALF), BF),
            pltpu.VMEM((last, 2, 4, 2, prow, HALF), BF),
            pltpu.VMEM((last, n_slot, HALF), BF),
            pltpu.VMEM((last, n_slot, HALF), BF),
            pltpu.VMEM((n_slot, 2 * ports), BF),
            pltpu.VMEM((2 * ports, n_slot), BF),
            pltpu.VMEM((n_row, other, scen), BF),
            pltpu.VMEM((ports + 128, scen), BF),
            pltpu.VMEM((n_row, ports + 128, scen), BF),
            pltpu.VMEM((n_row, rows + xr2, ports + 128), BF),
            pltpu.VMEM((xfs, 128), jnp.int32),
            pltpu.VMEM((n_row, xfs, 128), jnp.int32),
            pltpu.VMEM((rows + xr2, scen), F32),
            pltpu.VMEM((ports, scen), F32),
            pltpu.VMEM((ports, scen), F32),
            pltpu.VMEM((ports, scen), F32),
            dma((3,)),
            dma((9,)),
            dma((2, n_row)),
            dma((2, n_row)),
            dma((last, 2, 4, 2)),
            dma((last, 2, 4, 2)),
            dma((last,)),
            dma((last,)),
            dma((2, n_hop)),
            dma((2, n_hop)),
            dma((2, 4, 2)),
            dma((2, 4, 2)),
            dma((n_row,)),
            dma((n_row,)),
        ],
        compiler_params=pltpu.CompilerParams(
            collective_id=0, has_side_effects=True, vmem_limit_bytes=63 * 2**20
        ),
        name="grid_steps",
    )(
        source.reshape(steps, rows, scen),
        inverse_z.reshape(rows, nodes),
        pattern.reshape(pattern.shape[1:]),
        jnp.swapaxes(line_far.reshape(ports, 2), 0, 1),
        delay,
        xf_node,
        wave0.reshape(2, ports, scen),
        flux0.reshape(xfs, scen),
        volt0.reshape(xfs, scen),
        slope,
        knee,
    )
    return (voltage[None], flux[None])


def solution(mesh):
    return jax.shard_map(
        body,
        mesh=mesh,
        in_specs=(
            P(None, "sub", "row", None),
            P("sub", "row", None),
            P("sub", "row", None),
            P("sub", "row", None),
            P("sub", "row"),
            P("sub", "row"),
            P(None, "sub", "row", None),
            P("sub", "row", None),
            P("sub", "row", None),
            P(),
            P(),
        ),
        out_specs=(P("sub", "row", None), P("sub", "row", None)),
        check_vma=False,
    )
```

```python
import functools

import jax
import jax.numpy as jnp
from jax import lax
from jax.experimental import pallas as pl
from jax.experimental.pallas import tpu as pltpu
from jax.sharding import PartitionSpec as P

MESH = pl.DeviceIdType.MESH
BF = jnp.bfloat16
F32 = jnp.float32
HALF = 128
SLOTS = 8


def dot(a, b):
    return jnp.dot(a, b, preferred_element_type=F32)


def dot_t(a, b):
    return lax.dot_general(a, b, (((1,), (1,)), ((), ())), preferred_element_type=F32)


def kernel(
    n_sub, n_row, rows, ports, xfs, steps, block,
    source, z, pattern_in, far_in, delay_in, xf_in, wave0_in, flux0_in, volt0_in, slope_in, knee_in,
    vout, fout,
    pattern, far, delay, xf, wave0, flux0, volt0, slope, knee,
    zm, src, zxs, zc, zcx, zd, stat, y, rs_send, rs_recv, xs, xr, pk, un, s3, dyn, d3, zl, xfi, xfr, vacc, wrec, wear, warr,
    load_sem, in_sem, z_send, z_recv, rs_ssem, rs_rsem, x_ssem, x_rsem, s3_ssem, s3_rsem, d3_ssem, d3_rsem, i_ssem, i_rsem,
):
    me = lax.axis_index("row")
    sub = lax.axis_index("sub")
    last = steps - 1
    other = rows - ports
    xr2 = 2 * xfs
    prow = ports + xr2
    n_hop = n_row // 2

    def row_of(d):
        return lax.rem(me + d + 2 * n_row, n_row)

    def at_row(d):
        return (sub, row_of(d))

    def remote(a, b, ss, rs, dev):
        return pltpu.make_async_remote_copy(
            src_ref=a, dst_ref=b, send_sem=ss, recv_sem=rs, device_id=dev, device_id_type=MESH
        )

    def arrived(buf, rs):
        remote(buf, buf, rs, rs, at_row(1)).wait_recv()

    peers = sorted(range(1, n_sub), key=lambda i: -sum((0, 1, 2, 1)[(i >> b) & 3] for b in range(1, n_sub.bit_length(), 2)))
    order = []
    for d in range(n_hop - 1, 0, -1):
        order += [d, n_row - d] + ([n_hop] if d == n_hop - 1 else [])

    def peer(i):
        return jnp.bitwise_xor(sub, i)

    ld_z = pltpu.make_async_copy(z, zm.at[pl.ds(0, rows)], load_sem.at[0])
    ld_src = pltpu.make_async_copy(source, src, load_sem.at[1])
    small = [
        pltpu.make_async_copy(a, b, in_sem.at[i])
        for i, (a, b) in enumerate(
            [
                (pattern_in, pattern), (xf_in, xf), (far_in, far), (delay_in, delay), (wave0_in, wave0),
                (flux0_in, flux0), (volt0_in, volt0), (slope_in, slope), (knee_in, knee),
            ]
        )
    ]
    barrier = pltpu.get_barrier_semaphore()
    for i in peers:
        pl.semaphore_signal(barrier, inc=1, device_id=(peer(i), me), device_id_type=MESH)
    for d in order:
        pl.semaphore_signal(barrier, inc=1, device_id=at_row(d), device_id_type=MESH)
    for cp in small[:2]:
        cp.start()
    ld_z.start()
    ld_src.start()
    for cp in small[2:]:
        cp.start()

    for cp in small[:2]:
        cp.wait()
    bi = lax.broadcasted_iota(jnp.int32, (2 * xfs, 128), 0)
    idx = jnp.zeros((2 * xfs, 128), jnp.int32)
    for j in range(xfs):
        idx = jnp.where(bi == j, xf[0, j] & (rows - 1), idx)
    for c in range(n_row):
        v = idx
        for b in range(rows // block):
            v = jnp.where(bi == xfs + b, pattern[0, c * (rows // block) + b], v)
        xfi[c] = v

    pl.semaphore_wait(barrier, n_row - 1 + n_sub - 1)

    z_copies = []
    port_copies = []
    tail = list(order)

    def next_ports():
        if len(port_copies) >= 3:
            port_copies[-3].wait_send()
        d = tail.pop(0)
        cols = pl.ds(pl.multiple_of(row_of(d) * rows, rows), rows)
        cp = remote(z.at[pl.ds(0, ports), cols], zc.at[me, pl.ds(0, ports)], z_send.at[0, d], z_recv.at[0, d], at_row(d))
        cp.start()
        port_copies.append(cp)

    for d in order:
        cp = remote(xfi.at[row_of(d)], xfr.at[me], i_ssem.at[d], i_rsem.at[d], at_row(d))
        cp.start()
        z_copies.append(cp)
    for _ in range(3):
        next_ports()
    xfr[me] = xfi[me]

    ri = lax.broadcasted_iota(jnp.int32, (xr2, rows), 0)
    li = lax.broadcasted_iota(jnp.int32, (xr2, rows), 1)
    oh = jnp.zeros((xr2, rows), F32)
    lane = lax.broadcasted_iota(jnp.int32, (1, xfs), 1)
    node_row = jnp.zeros((1, xfs), jnp.int32)
    for j in range(xfs):
        node = xf[0, j] & (rows - 1)
        oh = jnp.where((lax.rem(ri, xfs) == j) & (li == node), 1.0, oh)
        node_row = jnp.where(lane == j, node, node_row)
    oh_cols = jnp.concatenate([oh, jnp.zeros((128 - xr2, rows), F32)], axis=0).astype(BF)
    oh = oh.astype(BF)
    shared = idx[0:xfs, 0:1] == node_row
    ahead = lax.broadcasted_iota(jnp.int32, (xfs, xfs), 1) < lax.broadcasted_iota(jnp.int32, (xfs, xfs), 0)
    first = jnp.sum(jnp.where(shared & ahead, 1, 0), axis=1, keepdims=True) == 0

    ld_z.wait()
    for brow in range(rows // block):

        def mask(b, c, brow=brow):
            m = jnp.where(pattern[brow, b] > 0, 1.0, 0.0).astype(F32)
            mv = jnp.full((1, block), m, F32).astype(BF)
            at = (pl.ds(brow * block, block), pl.ds(pl.multiple_of(b * block, block), block))
            zm[at] = zm[at] * mv
            return c

        lax.fori_loop(0, n_row * rows // block, mask, 0)

    def pick(c, carry):
        cols = pl.ds(pl.multiple_of(c * rows, rows), rows)
        v = dot(oh, zm[0:rows, cols])
        zm[rows : rows + xr2, cols] = v.astype(BF)
        zxs[c] = jnp.concatenate([v[0:xfs, 0 : rows // 2], v[0:xfs, rows // 2 :]], axis=0).astype(BF)
        return carry

    lax.fori_loop(0, n_row, pick, 0)
    for d in order:
        cp = remote(zxs.at[row_of(d)], zcx.at[me], z_send.at[1, d], z_recv.at[1, d], at_row(d))
        cp.start()
        z_copies.append(cp)

    for cp in small[2:]:
        cp.wait()
    eye = lax.broadcasted_iota(jnp.int32, (ports, ports), 0) == lax.broadcasted_iota(jnp.int32, (ports, ports), 1)
    before = lax.broadcasted_iota(jnp.int32, (ports, ports), 0) < lax.broadcasted_iota(jnp.int32, (ports, ports), 1)
    fs_row = far[0:1, :]
    fp_row = far[1:2, :]
    fs_col = jnp.sum(jnp.where(eye, fs_row, 0), axis=1, keepdims=True)
    fp_col = jnp.sum(jnp.where(eye, fp_row, 0), axis=1, keepdims=True)
    same = fs_col == fs_row
    rank_row = jnp.sum(jnp.where(same & before, 1, 0), axis=0, keepdims=True)
    rank_col = jnp.sum(jnp.where(same & (fp_row < fp_col), 1, 0), axis=1, keepdims=True)
    dl_col = jnp.sum(jnp.where(eye, delay[...], 0), axis=1, keepdims=True)
    late = dl_col == 2
    n_slot = 2 * SLOTS * n_sub
    place_row = fs_row * (2 * SLOTS) + rank_row
    place_col = fs_col * (2 * SLOTS) + rank_col
    for h in range(2):
        pi = lax.broadcasted_iota(jnp.int32, (n_slot, ports), 0)
        pk[:, h * ports : (h + 1) * ports] = jnp.where(pi == place_row + h * SLOTS, 1.0, 0.0).astype(BF)
        ui = lax.broadcasted_iota(jnp.int32, (ports, n_slot), 1)
        un[h * ports : (h + 1) * ports, :] = jnp.where(ui == place_col + h * SLOTS, 1.0, 0.0).astype(BF)
    own_slots = pl.ds(pl.multiple_of(sub * 2 * SLOTS, 2 * SLOTS), 2 * SLOTS)
    for t in range(last):
        xr[t, own_slots, :] = jnp.zeros((2 * SLOTS, HALF), BF)

    wrec[...] = wave0[0].astype(F32)
    wear[...] = wave0[1].astype(F32)
    dyn[...] = jnp.zeros_like(dyn)
    for c in range(n_row):
        d3[c, prow:] = jnp.zeros((d3.shape[1] - prow, d3.shape[2]), BF)

    def currents(flux, at_xf):
        total = slope[0] * flux
        for level in range(3):
            total = total + slope[level + 1] * (
                jnp.maximum(flux - knee[level], 0.0) + jnp.minimum(flux + knee[level], 0.0)
            )
        absorbed = jnp.zeros_like(total)
        for j in range(xfs):
            absorbed = absorbed + jnp.where(shared[:, j : j + 1], total[j : j + 1], 0.0)
        inject = (at_xf - absorbed).astype(BF).astype(F32)
        delta = jnp.where(first, inject - at_xf, 0.0)
        high = delta.astype(BF).astype(F32)
        return jnp.concatenate([high, delta - high], axis=0).astype(BF)

    ld_src.wait()
    at_xf = [dot(oh, src[t])[0:xfs] for t in range(steps)]

    def begin(t, flux):
        warr[...] = jnp.where(late, wear[...], wrec[...])
        cur = currents(flux, at_xf[t])
        if t < last:
            dyn[0:ports] = warr[...].astype(BF)
            dyn[ports:prow] = cur
        else:
            d3[me, 0:ports] = (src[last, 0:ports, :].astype(F32) + warr[...]).astype(BF)
            d3[me, ports:prow] = cur

    flux = flux0[...]
    xprev = volt0[...]
    begin(0, flux)

    zc[me, 0:ports] = zm[0:ports, pl.ds(pl.multiple_of(me * rows, rows), rows)]
    zcx[me] = zxs[me]
    s3[me] = src[last, ports:rows, :]

    def products(r):
        v = zcx[r].astype(F32)
        v = jnp.concatenate([v[0:xfs], v[xfs:]], axis=1)
        zc[r, ports:prow] = jnp.concatenate([v, jnp.zeros_like(v)], axis=0).astype(BF)
        keep = [jnp.where(xfr[r, xfs + b : xfs + b + 1] > 0, 1.0, 0.0) for b in range(rows // block)]
        keep = jnp.concatenate([k for k in keep for _ in range(block // 128)], axis=1).astype(BF)
        zc[r, 0:ports] = zc[r, 0:ports] * keep
        zr = zc[r]
        zd[r, :, 0:ports] = zc[r, :, 0:ports]
        zd[r, :, ports:] = dot_t(zr, oh_cols).astype(BF)
        y[r] = dot(zr, src[0]) + dot(zd[r], dyn[...])
        for t in range(1, last):
            stat[t - 1, r] = dot(zr, src[t])

    def add_dynamic(t, r):
        y[r] = stat[t - 1, r] + dot(zd[r], dyn[...])

    first_dir = jnp.where(lax.rem(me, n_hop) < n_hop // 2, 1, 0)

    def both_ways(f):
        for j in range(2):
            dirn = jnp.bitwise_xor(first_dir, j)
            f(dirn, 1 - 2 * dirn)

    def both(v):
        v = v.astype(F32)
        return v[0:xfs] + v[xfs:]

    sends = []

    def reduce_scatter(t, ready):
        def push(dirn, dest, slot, h, to, got):
            lanes = pl.ds(pl.multiple_of(h * HALF, HALF), HALF)
            acc_p = y[dest, 0:ports, lanes]
            acc_x = y[dest, ports : ports + xfs, lanes]
            for g in got:
                buf = rs_recv.at[t, dirn, g, h]
                arrived(buf, rs_rsem.at[t, dirn, g, h])
                acc_p = acc_p + buf[0:ports].astype(F32)
                acc_x = acc_x + both(buf[ports:prow])
            high = acc_x.astype(BF).astype(F32)
            rs_send[t, dirn, slot, h, 0:ports] = acc_p.astype(BF)
            rs_send[t, dirn, slot, h, ports:prow] = jnp.concatenate([high, acc_x - high], axis=0).astype(BF)
            cp = remote(
                rs_send.at[t, dirn, slot, h], rs_recv.at[t, dirn, slot, h],
                rs_ssem.at[t, dirn, slot, h], rs_rsem.at[t, dirn, slot, h], at_row(to),
            )
            cp.start()
            sends.append(cp)

        ready(4)
        both_ways(lambda dirn, sign: push(dirn, row_of(4 * sign), 0, dirn, 2 * sign, ()))
        ready(3)

        def second(dirn, sign):
            for h in range(2):
                push(dirn, row_of(3 * sign), 1, h, sign, ())

        both_ways(second)
        ready(2)

        def third(dirn, sign):
            push(dirn, row_of(2 * sign), 2, 1 - dirn, sign, (1,))
            push(dirn, row_of(2 * sign), 2, dirn, sign, (0, 1))

        both_ways(third)
        ready(1)

        def fourth(dirn, sign):
            for h in (1 - dirn, dirn):
                push(dirn, row_of(sign), 3, h, sign, (2,))

        both_ways(fourth)
        ready(0)
        at_ports, at_xfs = [], []
        for h in range(2):
            lanes = slice(h * HALF, (h + 1) * HALF)
            for dirn in range(2):
                arrived(rs_recv.at[t, dirn, 3, h], rs_rsem.at[t, dirn, 3, h])
            left, right = rs_recv.at[t, 0, 3, h], rs_recv.at[t, 1, 3, h]
            at_ports.append(y[me, 0:ports, lanes] + left[0:ports].astype(F32) + right[0:ports].astype(F32))
            at_xfs.append(y[me, ports : ports + xfs, lanes] + both(left[ports:prow]) + both(right[ports:prow]))
        return at_ports, at_xfs

    s3_cut = other // 2

    def s3_hop(k):
        for dirn in range(2):
            sign = 1 - 2 * dirn
            c = row_of(-sign * k)
            if k < n_hop - 1:
                part = pl.ds(0, other)
            else:
                part = pl.ds(dirn * s3_cut, s3_cut)
            cp = remote(s3.at[c, part], s3.at[c, part], s3_ssem.at[dirn, k], s3_rsem.at[dirn, k], at_row(sign))
            cp.start()
            sends.append(cp)

    def s3_wait(k):
        for dirn in range(2):
            part = pl.ds(0, other) if k < n_hop - 1 else pl.ds(0, s3_cut)
            arrived(s3.at[me, part], s3_rsem.at[dirn, k])

    def add_static(c):
        lo = pl.multiple_of(c * rows + ports, ports)
        vacc[...] += dot(zm[:, pl.ds(lo, other)], s3[c])

    def add_last(c):
        vacc[...] += dot(zl[c], d3[c])

    def columns(c, carry):
        node = xfr[c, 0:xfs, 0:1]
        hot = jnp.where(lax.broadcasted_iota(jnp.int32, (xfs, rows), 1) == node, 1.0, 0.0)
        hot = jnp.concatenate([hot, hot, jnp.zeros((128 - xr2, rows), F32)], axis=0).astype(BF)
        zl[c, :, 0:ports] = zm[:, pl.ds(pl.multiple_of(c * rows, rows), ports)]
        zl[c, :, ports:] = dot_t(zm[:, pl.ds(pl.multiple_of(c * rows, rows), rows)], hot).astype(BF)
        return carry

    products(me)
    vacc[...] = jnp.zeros_like(vacc)
    add_static(me)
    for d in range(1, n_row):
        arrived(xfr.at[row_of(-d)], i_rsem.at[d])
    lax.fori_loop(0, n_row, columns, 0)

    for t in range(last):

        def ready(d, t=t):
            if t == 0 and d == n_hop:
                for _ in range(2):
                    next_ports()
            if t == 0 and d == n_hop - 2:
                for _ in range(2):
                    next_ports()
            for e in (d, n_row - d) if 0 < d < n_hop else (d,):
                r = row_of(e)
                if t:
                    add_dynamic(t, r)
                elif e:
                    arrived(zc.at[r, pl.ds(0, ports)], z_recv.at[0, n_row - e])
                    arrived(zcx.at[r], z_recv.at[1, n_row - e])
                    products(r)

        at_ports, at_xfs = reduce_scatter(t, ready)
        xv = jnp.concatenate(at_xfs, axis=1)
        flux = flux + 0.5 * (xv + xprev)
        xprev = xv
        out = jnp.concatenate(
            [0.5 * at_ports[h] - warr[:, h * HALF : (h + 1) * HALF] for h in range(2)], axis=0
        ).astype(BF)
        xs[t] = dot(pk[...], out).astype(BF)
        for i in peers:
            p = peer(i)
            remote(
                xs.at[t, pl.ds(pl.multiple_of(p * 2 * SLOTS, 2 * SLOTS), 2 * SLOTS)],
                xr.at[t, own_slots],
                x_ssem.at[t],
                x_rsem.at[t],
                (p, me),
            ).start()
        if t:
            s3_wait(t - 1)
        s3_hop(t)
        if t:
            add_static(row_of(-t))
            add_static(row_of(t))
        total = pl.ds(0, (n_sub - 1) * 2 * SLOTS)
        pltpu.make_async_copy(xs.at[t, total], xr.at[t, total], x_rsem.at[t]).wait()
        inc = dot(un[...], xr[t])
        wear[...] = wrec[...]
        wrec[...] = jnp.concatenate([inc[0:ports], inc[ports : 2 * ports]], axis=1)
        begin(t + 1, flux)

    parts = ((0, ports // 2), (ports // 2, prow - ports // 2))

    def d3_send(dirn, sign, slot, p, c, to):
        part = pl.ds(*parts[p])
        cp = remote(d3.at[c, part], d3.at[c, part], d3_ssem.at[dirn, slot, p], d3_rsem.at[dirn, slot, p], at_row(to))
        cp.start()
        sends.append(cp)

    def d3_wait(dirn, slot, p):
        arrived(d3.at[me, pl.ds(*parts[p])], d3_rsem.at[dirn, slot, p])

    for p in range(2):
        both_ways(lambda dirn, sign: d3_send(dirn, sign, 0, p, me, sign))
    add_last(me)
    s3_wait(n_hop - 2)
    s3_hop(n_hop - 1)
    for k in (1, 2):

        def forward(dirn, sign):
            for p in range(2):
                d3_wait(dirn, k - 1, p)
                d3_send(dirn, sign, k, p, row_of(-sign * k), sign)
                if k == 2:
                    @pl.when(dirn == p)
                    def _():
                        part = pl.ds(*parts[p])
                        c = row_of(-sign * k)
                        remote(
                            d3.at[c, part], d3.at[c, part], d3_ssem.at[dirn, 3, p], d3_rsem.at[dirn, 3, p], at_row(2 * sign)
                        ).start()

        both_ways(forward)
        add_last(row_of(-k))
        add_last(row_of(k))
        if k == 1:
            add_static(row_of(-(n_hop - 1)))
            add_static(row_of(n_hop - 1))
    s3_wait(n_hop - 1)
    add_static(row_of(n_hop))
    for p in range(2):
        both_ways(lambda dirn, sign: d3_wait(dirn, 2, p))
    add_last(row_of(-3))
    add_last(row_of(3))
    for p in range(2):
        d3_wait(p, 3, p)
    add_last(row_of(n_hop))
    out_copy = pltpu.make_async_copy(vacc.at[pl.ds(0, rows)], vout, load_sem.at[0])
    out_copy.start()
    flux0[...] = flux + 0.5 * (vacc[rows : rows + xfs] + xprev)
    flux_copy = pltpu.make_async_copy(flux0, fout, load_sem.at[1])
    flux_copy.start()

    for cp in z_copies + port_copies[-3:] + sends:
        cp.wait_send()
    for p in range(2):
        buf = d3.at[me, pl.ds(*parts[p])]
        remote(buf, buf, d3_ssem.at[p, 3, p], d3_rsem.at[p, 3, p], at_row(1)).wait_send()
    for t in range(last):
        total = pl.ds(0, (n_sub - 1) * 2 * SLOTS)
        pltpu.make_async_copy(xs.at[t, total], xr.at[t, total], x_ssem.at[t]).wait()
    out_copy.wait()
    flux_copy.wait()


def hand_over(acc, flux_in, vout, fout):
    vout[...] = acc[...]
    fout[...] = flux_in[...]


def body(source, inverse_z, pattern, line_far, delay, xf_node, wave0, flux0, volt0, slope, knee):
    steps, _, rows, scen = source.shape
    nodes = inverse_z.shape[2]
    ports = line_far.shape[1]
    xfs = xf_node.shape[1]
    n_sub, n_row = lax.axis_size("sub"), lax.axis_size("row")
    block = nodes // pattern.shape[2]
    last = steps - 1
    xr2 = 2 * xfs
    prow = ports + xr2
    n_hop = n_row // 2
    other = rows - ports
    n_slot = 2 * SLOTS * n_sub
    hbm = pl.BlockSpec(memory_space=pltpu.HBM)
    dma = pltpu.SemaphoreType.DMA
    voltage, flux = pl.pallas_call(
        functools.partial(kernel, n_sub, n_row, rows, ports, xfs, steps, block),
        out_shape=(
            jax.ShapeDtypeStruct((rows, scen), F32),
            jax.ShapeDtypeStruct((xfs, scen), F32),
        ),
        in_specs=[hbm] * 11,
        out_specs=(hbm, hbm),
        scratch_shapes=[
            pltpu.SMEM(pattern.shape[1:], jnp.int32),
            pltpu.VMEM((2, ports), jnp.int32),
            pltpu.VMEM(delay.shape, jnp.int32),
            pltpu.SMEM(xf_node.shape, jnp.int32),
            pltpu.VMEM((2, ports, scen), BF),
            pltpu.VMEM((xfs, scen), F32),
            pltpu.VMEM((xfs, scen), F32),
            pltpu.SMEM(slope.shape, F32),
            pltpu.SMEM(knee.shape, F32),
            pltpu.VMEM((rows + xr2, nodes), BF),
            pltpu.VMEM((steps, rows, scen), BF),
            pltpu.VMEM((n_row, xr2, rows // 2), BF),
            pltpu.VMEM((n_row, prow, rows), BF),
            pltpu.VMEM((n_row, xr2, rows // 2), BF),
            pltpu.VMEM((n_row, prow, ports + 128), BF),
            pltpu.VMEM((last - 1, n_row, prow, scen), F32),
            pltpu.VMEM((n_row, prow, scen), F32),
            pltpu.VMEM((last, 2, 4, 2, prow, HALF), BF),
            pltpu.VMEM((last, 2, 4, 2, prow, HALF), BF),
            pltpu.VMEM((last, n_slot, HALF), BF),
            pltpu.VMEM((last, n_slot, HALF), BF),
            pltpu.VMEM((n_slot, 2 * ports), BF),
            pltpu.VMEM((2 * ports, n_slot), BF),
            pltpu.VMEM((n_row, other, scen), BF),
            pltpu.VMEM((ports + 128, scen), BF),
            pltpu.VMEM((n_row, ports + 128, scen), BF),
            pltpu.VMEM((n_row, rows + xr2, ports + 128), BF),
            pltpu.VMEM((n_row, 2 * xfs, 128), jnp.int32),
            pltpu.VMEM((n_row, 2 * xfs, 128), jnp.int32),
            pltpu.VMEM((rows + xr2, scen), F32),
            pltpu.VMEM((ports, scen), F32),
            pltpu.VMEM((ports, scen), F32),
            pltpu.VMEM((ports, scen), F32),
            dma((2,)),
            dma((9,)),
            dma((2, n_row)),
            dma((2, n_row)),
            dma((last, 2, 4, 2)),
            dma((last, 2, 4, 2)),
            dma((last,)),
            dma((last,)),
            dma((2, n_hop)),
            dma((2, n_hop)),
            dma((2, 4, 2)),
            dma((2, 4, 2)),
            dma((n_row,)),
            dma((n_row,)),
        ],
        compiler_params=pltpu.CompilerParams(
            collective_id=0, has_side_effects=True, vmem_limit_bytes=63 * 2**20
        ),
        name="grid_steps",
    )(
        source.reshape(steps, rows, scen),
        inverse_z.reshape(rows, nodes),
        pattern.reshape(pattern.shape[1:]),
        jnp.swapaxes(line_far.reshape(ports, 2), 0, 1),
        delay,
        xf_node,
        wave0.reshape(2, ports, scen),
        flux0.reshape(xfs, scen),
        volt0.reshape(xfs, scen),
        slope,
        knee,
    )
    vmem = pl.BlockSpec(memory_space=pltpu.VMEM)
    voltage, flux = pl.pallas_call(
        hand_over,
        out_shape=(
            jax.ShapeDtypeStruct((rows, scen), F32),
            jax.ShapeDtypeStruct((xfs, scen), F32),
        ),
        in_specs=[vmem] * 2,
        out_specs=(vmem, vmem),
        compiler_params=pltpu.CompilerParams(vmem_limit_bytes=63 * 2**20),
        name="hand_over",
    )(voltage, flux)
    return (voltage[None], flux[None])


def solution(mesh):
    return jax.shard_map(
        body,
        mesh=mesh,
        in_specs=(
            P(None, "sub", "row", None),
            P("sub", "row", None),
            P("sub", "row", None),
            P("sub", "row", None),
            P("sub", "row"),
            P("sub", "row"),
            P(None, "sub", "row", None),
            P("sub", "row", None),
            P("sub", "row", None),
            P(),
            P(),
        ),
        out_specs=(P("sub", "row", None), P("sub", "row", None)),
        check_vma=False,
    )
```

```python
import functools

import jax
import jax.numpy as jnp
from jax import lax
from jax.experimental import pallas as pl
from jax.experimental.pallas import tpu as pltpu
from jax.sharding import PartitionSpec as P

MESH = pl.DeviceIdType.MESH
BF = jnp.bfloat16
F32 = jnp.float32
HALF = 128
SLOTS = 8


def dot(a, b):
    return jnp.dot(a, b, preferred_element_type=F32)


def dot_t(a, b):
    return lax.dot_general(a, b, (((1,), (1,)), ((), ())), preferred_element_type=F32)


def kernel(
    n_sub, n_row, rows, ports, xfs, steps, block,
    source, z, pattern_in, far_in, delay_in, xf_in, wave0_in, flux0_in, volt0_in, slope_in, knee_in,
    vout, fout,
    pattern, far, delay, xf, wave0, flux0, volt0, slope, knee,
    zm, src, zxs, zc, zcx, zd, stat, y, rs_send, rs_recv, xs, xr, pk, un, s3, dyn, d3, zl, xfi, xfr, vacc, wrec, wear, warr,
    load_sem, in_sem, z_send, z_recv, rs_ssem, rs_rsem, x_ssem, x_rsem, s3_ssem, s3_rsem, d3_ssem, d3_rsem, i_ssem, i_rsem,
):
    me = lax.axis_index("row")
    sub = lax.axis_index("sub")
    last = steps - 1
    other = rows - ports
    xr2 = 2 * xfs
    prow = ports + xr2
    n_hop = n_row // 2

    def row_of(d):
        return lax.rem(me + d + 2 * n_row, n_row)

    def at_row(d):
        return (sub, row_of(d))

    def remote(a, b, ss, rs, dev):
        return pltpu.make_async_remote_copy(
            src_ref=a, dst_ref=b, send_sem=ss, recv_sem=rs, device_id=dev, device_id_type=MESH
        )

    def arrived(buf, rs):
        remote(buf, buf, rs, rs, at_row(1)).wait_recv()

    peers = sorted(range(1, n_sub), key=lambda i: -sum((0, 1, 2, 1)[(i >> b) & 3] for b in range(1, n_sub.bit_length(), 2)))
    order = []
    for d in range(n_hop - 1, 0, -1):
        order += [d, n_row - d] + ([n_hop] if d == n_hop - 1 else [])

    def peer(i):
        return jnp.bitwise_xor(sub, i)

    ld_z = pltpu.make_async_copy(z, zm.at[pl.ds(0, rows)], load_sem.at[0])
    ld_src = pltpu.make_async_copy(source, src, load_sem.at[1])
    small = [
        pltpu.make_async_copy(a, b, in_sem.at[i])
        for i, (a, b) in enumerate(
            [
                (pattern_in, pattern), (xf_in, xf), (far_in, far), (delay_in, delay), (wave0_in, wave0),
                (flux0_in, flux0), (volt0_in, volt0), (slope_in, slope), (knee_in, knee),
            ]
        )
    ]
    barrier = pltpu.get_barrier_semaphore()
    for i in peers:
        pl.semaphore_signal(barrier, inc=1, device_id=(peer(i), me), device_id_type=MESH)
    for d in order:
        pl.semaphore_signal(barrier, inc=1, device_id=at_row(d), device_id_type=MESH)
    for cp in small[:2]:
        cp.start()
    ld_z.start()
    ld_src.start()
    for cp in small[2:]:
        cp.start()

    for cp in small[:2]:
        cp.wait()
    bi = lax.broadcasted_iota(jnp.int32, (2 * xfs, 128), 0)
    idx = jnp.zeros((2 * xfs, 128), jnp.int32)
    for j in range(xfs):
        idx = jnp.where(bi == j, xf[0, j] & (rows - 1), idx)
    for c in range(n_row):
        v = idx
        for b in range(rows // block):
            v = jnp.where(bi == xfs + b, pattern[0, c * (rows // block) + b], v)
        xfi[c] = v

    pl.semaphore_wait(barrier, n_row - 1 + n_sub - 1)

    z_copies = []
    port_copies = []
    tail = list(order)

    def next_ports():
        if len(port_copies) >= 3:
            port_copies[-3].wait_send()
        d = tail.pop(0)
        cols = pl.ds(pl.multiple_of(row_of(d) * rows, rows), rows)
        cp = remote(z.at[pl.ds(0, ports), cols], zc.at[me, pl.ds(0, ports)], z_send.at[0, d], z_recv.at[0, d], at_row(d))
        cp.start()
        port_copies.append(cp)

    for d in order:
        cp = remote(xfi.at[row_of(d)], xfr.at[me], i_ssem.at[d], i_rsem.at[d], at_row(d))
        cp.start()
        z_copies.append(cp)
    for _ in range(3):
        next_ports()
    xfr[me] = xfi[me]

    ri = lax.broadcasted_iota(jnp.int32, (xr2, rows), 0)
    li = lax.broadcasted_iota(jnp.int32, (xr2, rows), 1)
    oh = jnp.zeros((xr2, rows), F32)
    lane = lax.broadcasted_iota(jnp.int32, (1, xfs), 1)
    node_row = jnp.zeros((1, xfs), jnp.int32)
    for j in range(xfs):
        node = xf[0, j] & (rows - 1)
        oh = jnp.where((lax.rem(ri, xfs) == j) & (li == node), 1.0, oh)
        node_row = jnp.where(lane == j, node, node_row)
    oh_cols = jnp.concatenate([oh, jnp.zeros((128 - xr2, rows), F32)], axis=0).astype(BF)
    oh = oh.astype(BF)
    shared = idx[0:xfs, 0:1] == node_row
    ahead = lax.broadcasted_iota(jnp.int32, (xfs, xfs), 1) < lax.broadcasted_iota(jnp.int32, (xfs, xfs), 0)
    first = jnp.sum(jnp.where(shared & ahead, 1, 0), axis=1, keepdims=True) == 0

    ld_z.wait()
    for brow in range(rows // block):

        def mask(b, c, brow=brow):
            m = jnp.where(pattern[brow, b] > 0, 1.0, 0.0).astype(F32)
            mv = jnp.full((1, block), m, F32).astype(BF)
            at = (pl.ds(brow * block, block), pl.ds(pl.multiple_of(b * block, block), block))
            zm[at] = zm[at] * mv
            return c

        lax.fori_loop(0, n_row * rows // block, mask, 0)

    def pick(c, carry):
        cols = pl.ds(pl.multiple_of(c * rows, rows), rows)
        v = dot(oh, zm[0:rows, cols])
        zm[rows : rows + xr2, cols] = v.astype(BF)
        zxs[c] = jnp.concatenate([v[0:xfs, 0 : rows // 2], v[0:xfs, rows // 2 :]], axis=0).astype(BF)
        return carry

    lax.fori_loop(0, n_row, pick, 0)
    for d in order:
        cp = remote(zxs.at[row_of(d)], zcx.at[me], z_send.at[1, d], z_recv.at[1, d], at_row(d))
        cp.start()
        z_copies.append(cp)

    for cp in small[2:]:
        cp.wait()
    eye = lax.broadcasted_iota(jnp.int32, (ports, ports), 0) == lax.broadcasted_iota(jnp.int32, (ports, ports), 1)
    before = lax.broadcasted_iota(jnp.int32, (ports, ports), 0) < lax.broadcasted_iota(jnp.int32, (ports, ports), 1)
    fs_row = far[0:1, :]
    fp_row = far[1:2, :]
    fs_col = jnp.sum(jnp.where(eye, fs_row, 0), axis=1, keepdims=True)
    fp_col = jnp.sum(jnp.where(eye, fp_row, 0), axis=1, keepdims=True)
    same = fs_col == fs_row
    rank_row = jnp.sum(jnp.where(same & before, 1, 0), axis=0, keepdims=True)
    rank_col = jnp.sum(jnp.where(same & (fp_row < fp_col), 1, 0), axis=1, keepdims=True)
    dl_col = jnp.sum(jnp.where(eye, delay[...], 0), axis=1, keepdims=True)
    late = dl_col == 2
    n_slot = 2 * SLOTS * n_sub
    place_row = fs_row * (2 * SLOTS) + rank_row
    place_col = fs_col * (2 * SLOTS) + rank_col
    for h in range(2):
        pi = lax.broadcasted_iota(jnp.int32, (n_slot, ports), 0)
        pk[:, h * ports : (h + 1) * ports] = jnp.where(pi == place_row + h * SLOTS, 1.0, 0.0).astype(BF)
        ui = lax.broadcasted_iota(jnp.int32, (ports, n_slot), 1)
        un[h * ports : (h + 1) * ports, :] = jnp.where(ui == place_col + h * SLOTS, 1.0, 0.0).astype(BF)
    own_slots = pl.ds(pl.multiple_of(sub * 2 * SLOTS, 2 * SLOTS), 2 * SLOTS)
    for t in range(last):
        xr[t, own_slots, :] = jnp.zeros((2 * SLOTS, HALF), BF)

    wrec[...] = wave0[0].astype(F32)
    wear[...] = wave0[1].astype(F32)
    dyn[...] = jnp.zeros_like(dyn)
    for c in range(n_row):
        d3[c, prow:] = jnp.zeros((d3.shape[1] - prow, d3.shape[2]), BF)

    def currents(flux, at_xf):
        total = slope[0] * flux
        for level in range(3):
            total = total + slope[level + 1] * (
                jnp.maximum(flux - knee[level], 0.0) + jnp.minimum(flux + knee[level], 0.0)
            )
        absorbed = jnp.zeros_like(total)
        for j in range(xfs):
            absorbed = absorbed + jnp.where(shared[:, j : j + 1], total[j : j + 1], 0.0)
        inject = (at_xf - absorbed).astype(BF).astype(F32)
        delta = jnp.where(first, inject - at_xf, 0.0)
        high = delta.astype(BF).astype(F32)
        return jnp.concatenate([high, delta - high], axis=0).astype(BF)

    ld_src.wait()
    at_xf = [dot(oh, src[t])[0:xfs] for t in range(steps)]

    def begin(t, flux):
        warr[...] = jnp.where(late, wear[...], wrec[...])
        cur = currents(flux, at_xf[t])
        if t < last:
            dyn[0:ports] = warr[...].astype(BF)
            dyn[ports:prow] = cur
        else:
            d3[me, 0:ports] = (src[last, 0:ports, :].astype(F32) + warr[...]).astype(BF)
            d3[me, ports:prow] = cur

    flux = flux0[...]
    xprev = volt0[...]
    begin(0, flux)

    zc[me, 0:ports] = zm[0:ports, pl.ds(pl.multiple_of(me * rows, rows), rows)]
    zcx[me] = zxs[me]
    s3[me] = src[last, ports:rows, :]

    places = [n_hop]
    for d in range(n_hop - 1, 0, -1):
        places += [d, n_row - d]
    places += [0]

    def block_at(i):
        return pl.ds(pl.multiple_of(i * prow, 16), prow)

    def products(i):
        r = row_of(places[i])
        keep = [jnp.where(xfr[r, xfs + b : xfs + b + 1] > 0, 1.0, 0.0) for b in range(rows // block)]
        keep = jnp.concatenate([k for k in keep for _ in range(block // 128)], axis=1).astype(BF)
        zc[r, 0:ports] = zc[r, 0:ports] * keep
        v = zcx[r].astype(F32)
        v = jnp.concatenate([v[0:xfs], v[xfs:]], axis=1)
        zc[r, ports:prow] = jnp.concatenate([v, jnp.zeros_like(v)], axis=0).astype(BF)
        zr = zc[r]
        zd[block_at(i), 0:ports] = zc[r, :, 0:ports]
        zd[block_at(i), ports:] = dot_t(zr, oh_cols).astype(BF)
        y[block_at(i)] = dot(zr, src[0]) + dot(zd[block_at(i)], dyn[...])

    def static_products(i):
        zr = zc[row_of(places[i])]
        for t in range(1, last):
            stat[t - 1, block_at(i)] = dot(zr, src[t])

    def add_dynamic(t, lo, hi):
        at = pl.ds(lo * prow, (hi - lo) * prow)
        y[at] = stat[t - 1, at] + dot(zd[at], dyn[...])

    first_dir = jnp.where(lax.rem(me, n_hop) < n_hop // 2, 1, 0)

    def both_ways(f):
        for j in range(2):
            dirn = jnp.bitwise_xor(first_dir, j)
            f(dirn, 1 - 2 * dirn)

    def both(v):
        v = v.astype(F32)
        return v[0:xfs] + v[xfs:]

    sends = []

    def reduce_scatter(t, ready):
        def push(dirn, k, slot, h, to, got):
            lanes = pl.ds(pl.multiple_of(h * HALF, HALF), HALF)
            place = 0 if k == n_hop else 1 + 2 * (n_hop - 1 - k) + dirn
            lo = pl.multiple_of(place * prow, 16)
            acc_p = y[pl.ds(lo, ports), lanes]
            acc_x = y[pl.ds(pl.multiple_of(lo + ports, 16), xfs), lanes]
            for g in got:
                buf = rs_recv.at[t, dirn, g, h]
                arrived(buf, rs_rsem.at[t, dirn, g, h])
                acc_p = acc_p + buf[0:ports].astype(F32)
                acc_x = acc_x + both(buf[ports:prow])
            high = acc_x.astype(BF).astype(F32)
            rs_send[t, dirn, slot, h, 0:ports] = acc_p.astype(BF)
            rs_send[t, dirn, slot, h, ports:prow] = jnp.concatenate([high, acc_x - high], axis=0).astype(BF)
            cp = remote(
                rs_send.at[t, dirn, slot, h], rs_recv.at[t, dirn, slot, h],
                rs_ssem.at[t, dirn, slot, h], rs_rsem.at[t, dirn, slot, h], at_row(to),
            )
            cp.start()
            sends.append(cp)

        far_to = 2

        def first_leg(dirn, sign):
            push(dirn, 4, 0, dirn, far_to * sign, ())

        def second(dirn, sign):
            if far_to == 1:
                push(dirn, 3, 1, 1 - dirn, sign, ())
                push(dirn, 3, 1, dirn, sign, (0,))
            else:
                for h in range(2):
                    push(dirn, 3, 1, h, sign, ())

        def third(dirn, sign):
            push(dirn, 2, 2, 1 - dirn, sign, (1,))
            push(dirn, 2, 2, dirn, sign, (1,) if far_to == 1 else (0, 1))

        def fourth(dirn, sign):
            for h in (1 - dirn, dirn):
                push(dirn, 1, 3, h, sign, (2,))

        ready(0)
        both_ways(first_leg)
        ready(1)
        both_ways(second)
        ready(2)
        both_ways(third)
        ready(3)
        both_ways(fourth)
        ready(4)
        own = (n_row - 1) * prow
        at_ports, at_xfs = [], []
        for h in range(2):
            lanes = slice(h * HALF, (h + 1) * HALF)
            for dirn in range(2):
                arrived(rs_recv.at[t, dirn, 3, h], rs_rsem.at[t, dirn, 3, h])
            left, right = rs_recv.at[t, 0, 3, h], rs_recv.at[t, 1, 3, h]
            at_ports.append(y[own : own + ports, lanes] + left[0:ports].astype(F32) + right[0:ports].astype(F32))
            at_xfs.append(y[own + ports : own + ports + xfs, lanes] + both(left[ports:prow]) + both(right[ports:prow]))
        return at_ports, at_xfs

    s3_cut = other // 2

    def s3_hop(k):
        for dirn in range(2):
            sign = 1 - 2 * dirn
            c = row_of(-sign * k)
            if k < n_hop - 1:
                part = pl.ds(0, other)
            else:
                part = pl.ds(dirn * s3_cut, s3_cut)
            cp = remote(s3.at[c, part], s3.at[c, part], s3_ssem.at[dirn, k], s3_rsem.at[dirn, k], at_row(sign))
            cp.start()
            sends.append(cp)

    def s3_wait(k):
        for dirn in range(2):
            part = pl.ds(0, other) if k < n_hop - 1 else pl.ds(0, s3_cut)
            arrived(s3.at[me, part], s3_rsem.at[dirn, k])

    def add_static(c):
        lo = pl.multiple_of(c * rows + ports, ports)
        vacc[...] += dot(zm[:, pl.ds(lo, other)], s3[c])

    def add_last(c):
        vacc[...] += dot(zl[c], d3[c])

    def columns(c, carry):
        node = xfr[c, 0:xfs, 0:1]
        hot = jnp.where(lax.broadcasted_iota(jnp.int32, (xfs, rows), 1) == node, 1.0, 0.0)
        hot = jnp.concatenate([hot, hot, jnp.zeros((128 - xr2, rows), F32)], axis=0).astype(BF)
        zl[c, :, 0:ports] = zm[:, pl.ds(pl.multiple_of(c * rows, rows), ports)]
        zl[c, :, ports:] = dot_t(zm[:, pl.ds(pl.multiple_of(c * rows, rows), rows)], hot).astype(BF)
        return carry

    products(n_row - 1)
    static_products(n_row - 1)
    vacc[...] = jnp.zeros_like(vacc)
    add_static(me)
    for d in range(1, n_row):
        arrived(xfr.at[row_of(-d)], i_rsem.at[d])
    lax.fori_loop(0, n_row, columns, 0)

    for t in range(last):

        def ready(stage, t=t):
            if t:
                if stage == 0:
                    add_dynamic(t, 0, 3)
                elif stage == 1:
                    add_dynamic(t, 3, n_row)
                return
            if stage > 0:
                for i in (0,) if stage == 1 else (2 * stage - 3, 2 * stage - 2):
                    static_products(i)
            if stage in (0, 2):
                for _ in range(2):
                    next_ports()
            for i in (0,) if stage == 0 else (2 * stage - 1, 2 * stage) if stage < 4 else ():
                e = places[i]
                r = row_of(e)
                arrived(zc.at[r, pl.ds(0, ports)], z_recv.at[0, n_row - e])
                arrived(zcx.at[r], z_recv.at[1, n_row - e])
                products(i)

        at_ports, at_xfs = reduce_scatter(t, ready)
        xv = jnp.concatenate(at_xfs, axis=1)
        flux = flux + 0.5 * (xv + xprev)
        xprev = xv
        out = jnp.concatenate(
            [0.5 * at_ports[h] - warr[:, h * HALF : (h + 1) * HALF] for h in range(2)], axis=0
        ).astype(BF)
        xs[t] = dot(pk[...], out).astype(BF)
        for i in peers:
            p = peer(i)
            remote(
                xs.at[t, pl.ds(pl.multiple_of(p * 2 * SLOTS, 2 * SLOTS), 2 * SLOTS)],
                xr.at[t, own_slots],
                x_ssem.at[t],
                x_rsem.at[t],
                (p, me),
            ).start()
        if t:
            s3_wait(t - 1)
        s3_hop(t)
        if t:
            add_static(row_of(-t))
            add_static(row_of(t))
        total = pl.ds(0, (n_sub - 1) * 2 * SLOTS)
        pltpu.make_async_copy(xs.at[t, total], xr.at[t, total], x_rsem.at[t]).wait()
        inc = dot(un[...], xr[t])
        wear[...] = wrec[...]
        wrec[...] = jnp.concatenate([inc[0:ports], inc[ports : 2 * ports]], axis=1)
        begin(t + 1, flux)

    parts = ((0, ports // 2), (ports // 2, prow - ports // 2))

    def d3_send(dirn, sign, slot, p, c, to):
        part = pl.ds(*parts[p])
        cp = remote(d3.at[c, part], d3.at[c, part], d3_ssem.at[dirn, slot, p], d3_rsem.at[dirn, slot, p], at_row(to))
        cp.start()
        sends.append(cp)

    def d3_wait(dirn, slot, p):
        arrived(d3.at[me, pl.ds(*parts[p])], d3_rsem.at[dirn, slot, p])

    for p in range(2):
        both_ways(lambda dirn, sign: d3_send(dirn, sign, 0, p, me, sign))
    add_last(me)
    s3_wait(n_hop - 2)
    s3_hop(n_hop - 1)
    for k in (1, 2):

        def forward(dirn, sign):
            for p in range(2):
                d3_wait(dirn, k - 1, p)
                d3_send(dirn, sign, k, p, row_of(-sign * k), sign)
                if k == 2:
                    @pl.when(dirn == p)
                    def _():
                        part = pl.ds(*parts[p])
                        c = row_of(-sign * k)
                        remote(
                            d3.at[c, part], d3.at[c, part], d3_ssem.at[dirn, 3, p], d3_rsem.at[dirn, 3, p], at_row(2 * sign)
                        ).start()

        both_ways(forward)
        add_last(row_of(-k))
        add_last(row_of(k))
        if k == 1:
            add_static(row_of(-(n_hop - 1)))
            add_static(row_of(n_hop - 1))
    s3_wait(n_hop - 1)
    add_static(row_of(n_hop))
    for p in range(2):
        both_ways(lambda dirn, sign: d3_wait(dirn, 2, p))
    add_last(row_of(-3))
    add_last(row_of(3))
    for p in range(2):
        d3_wait(p, 3, p)
    far_row = row_of(n_hop)
    piece = rows // 2
    outs = []
    for i in (1, 0):
        n = piece + xr2 * i
        vacc[i * piece : i * piece + n] += dot(zl[far_row, i * piece : i * piece + n], d3[far_row])
        at = pl.ds(i * piece, piece)
        cp = pltpu.make_async_copy(vacc.at[at], vout.at[at], load_sem.at[i])
        cp.start()
        outs.append(cp)
        if i:
            flux0[...] = flux + 0.5 * (vacc[rows : rows + xfs] + xprev)
            cp = pltpu.make_async_copy(flux0, fout, in_sem.at[0])
            cp.start()
            outs.append(cp)

    for cp in z_copies + port_copies[-3:] + sends:
        cp.wait_send()
    for p in range(2):
        buf = d3.at[me, pl.ds(*parts[p])]
        remote(buf, buf, d3_ssem.at[p, 3, p], d3_rsem.at[p, 3, p], at_row(1)).wait_send()
    for t in range(last):
        total = pl.ds(0, (n_sub - 1) * 2 * SLOTS)
        pltpu.make_async_copy(xs.at[t, total], xr.at[t, total], x_ssem.at[t]).wait()
    for cp in outs:
        cp.wait()


def hand_over(acc, flux_in, vout, fout):
    vout[...] = acc[...]
    fout[...] = flux_in[...]


def body(source, inverse_z, pattern, line_far, delay, xf_node, wave0, flux0, volt0, slope, knee):
    steps, _, rows, scen = source.shape
    nodes = inverse_z.shape[2]
    ports = line_far.shape[1]
    xfs = xf_node.shape[1]
    n_sub, n_row = lax.axis_size("sub"), lax.axis_size("row")
    block = nodes // pattern.shape[2]
    last = steps - 1
    xr2 = 2 * xfs
    prow = ports + xr2
    n_hop = n_row // 2
    other = rows - ports
    n_slot = 2 * SLOTS * n_sub
    hbm = pl.BlockSpec(memory_space=pltpu.HBM)
    dma = pltpu.SemaphoreType.DMA
    voltage, flux = pl.pallas_call(
        functools.partial(kernel, n_sub, n_row, rows, ports, xfs, steps, block),
        out_shape=(
            jax.ShapeDtypeStruct((rows, scen), F32),
            jax.ShapeDtypeStruct((xfs, scen), F32),
        ),
        in_specs=[hbm] * 11,
        out_specs=(hbm, hbm),
        scratch_shapes=[
            pltpu.SMEM(pattern.shape[1:], jnp.int32),
            pltpu.VMEM((2, ports), jnp.int32),
            pltpu.VMEM(delay.shape, jnp.int32),
            pltpu.SMEM(xf_node.shape, jnp.int32),
            pltpu.VMEM((2, ports, scen), BF),
            pltpu.VMEM((xfs, scen), F32),
            pltpu.VMEM((xfs, scen), F32),
            pltpu.SMEM(slope.shape, F32),
            pltpu.SMEM(knee.shape, F32),
            pltpu.VMEM((rows + xr2, nodes), BF),
            pltpu.VMEM((steps, rows, scen), BF),
            pltpu.VMEM((n_row, xr2, rows // 2), BF),
            pltpu.VMEM((n_row, prow, rows), BF),
            pltpu.VMEM((n_row, xr2, rows // 2), BF),
            pltpu.VMEM((n_row * prow, ports + 128), BF),
            pltpu.VMEM((last - 1, n_row * prow, scen), F32),
            pltpu.VMEM((n_row * prow, scen), F32),
            pltpu.VMEM((last, 2, 4, 2, prow, HALF), BF),
            pltpu.VMEM((last, 2, 4, 2, prow, HALF), BF),
            pltpu.VMEM((last, n_slot, HALF), BF),
            pltpu.VMEM((last, n_slot, HALF), BF),
            pltpu.VMEM((n_slot, 2 * ports), BF),
            pltpu.VMEM((2 * ports, n_slot), BF),
            pltpu.VMEM((n_row, other, scen), BF),
            pltpu.VMEM((ports + 128, scen), BF),
            pltpu.VMEM((n_row, ports + 128, scen), BF),
            pltpu.VMEM((n_row, rows + xr2, ports + 128), BF),
            pltpu.VMEM((n_row, 2 * xfs, 128), jnp.int32),
            pltpu.VMEM((n_row, 2 * xfs, 128), jnp.int32),
            pltpu.VMEM((rows + xr2, scen), F32),
            pltpu.VMEM((ports, scen), F32),
            pltpu.VMEM((ports, scen), F32),
            pltpu.VMEM((ports, scen), F32),
            dma((2,)),
            dma((9,)),
            dma((2, n_row)),
            dma((2, n_row)),
            dma((last, 2, 4, 2)),
            dma((last, 2, 4, 2)),
            dma((last,)),
            dma((last,)),
            dma((2, n_hop)),
            dma((2, n_hop)),
            dma((2, 4, 2)),
            dma((2, 4, 2)),
            dma((n_row,)),
            dma((n_row,)),
        ],
        compiler_params=pltpu.CompilerParams(
            collective_id=0, has_side_effects=True, vmem_limit_bytes=63 * 2**20
        ),
        name="grid_steps",
    )(
        source.reshape(steps, rows, scen),
        inverse_z.reshape(rows, nodes),
        pattern.reshape(pattern.shape[1:]),
        jnp.swapaxes(line_far.reshape(ports, 2), 0, 1),
        delay,
        xf_node,
        wave0.reshape(2, ports, scen),
        flux0.reshape(xfs, scen),
        volt0.reshape(xfs, scen),
        slope,
        knee,
    )
    vmem = pl.BlockSpec(memory_space=pltpu.VMEM)
    voltage, flux = pl.pallas_call(
        hand_over,
        out_shape=(
            jax.ShapeDtypeStruct((rows, scen), F32),
            jax.ShapeDtypeStruct((xfs, scen), F32),
        ),
        in_specs=[vmem] * 2,
        out_specs=(vmem, vmem),
        compiler_params=pltpu.CompilerParams(vmem_limit_bytes=63 * 2**20),
        name="hand_over",
    )(voltage, flux)
    return (voltage[None], flux[None])


def solution(mesh):
    return jax.shard_map(
        body,
        mesh=mesh,
        in_specs=(
            P(None, "sub", "row", None),
            P("sub", "row", None),
            P("sub", "row", None),
            P("sub", "row", None),
            P("sub", "row"),
            P("sub", "row"),
            P(None, "sub", "row", None),
            P("sub", "row", None),
            P("sub", "row", None),
            P(),
            P(),
        ),
        out_specs=(P("sub", "row", None), P("sub", "row", None)),
        check_vma=False,
    )
```
